256 devices in a mesh: dp: 8 (over x, z_lo), ctx: 32 (over y, z_hi, core).
Axes of the slice: x: 4, y: 4, z: 8 (z_hi: 4, z_lo: 2; z = z_hi * 2 + z_lo), core: 2. Of those that a mesh axis runs over, the one named last changes fastest.
Arguments:
- query_gate: bfloat16 [8, 4096, 2048], P('dp', 'ctx'), may hold values from -6 to 6
- key_gate: bfloat16 [8, 4096, 2048], P('dp', 'ctx'), may hold values from -6 to 6
- value_in: bfloat16 [8, 4096, 2048], P('dp', 'ctx'), may hold values from -6 to 6
- out_grad: bfloat16 [8, 4096, 2048], P('dp', 'ctx'), may hold values from -6 to 6
- filter_taps: float32 [2048, 4096], P('ctx'), may hold values from -2 to 2
Outputs:
- mixed_out: bfloat16 [8, 4096, 2048], P('dp', 'ctx')
- query_grad: bfloat16 [8, 4096, 2048], P('dp', 'ctx')
- key_grad: bfloat16 [8, 4096, 2048], P('dp', 'ctx')
- value_grad: bfloat16 [8, 4096, 2048], P('dp', 'ctx')
- filter_grad: float32 [2048, 4096], P('ctx', 'dp')
The draws below stay inside these ranges and needn't reach their ends.
All inputs are finite; a program needn't handle non-finite values.
Results may differ from the reference program's by a relative error of at most 0.017.
Values may be sent and summed in bfloat16 or wider, within the bound.
A program may use at most 128 MiB of HBM per device.

```python
import math
import jax
import jax.numpy as jnp
from jax import lax

CHANNEL_GROUP = 2048
SEQUENCE_LENGTH = 4096
SEQS = 8


def draw_filter_taps(key, part):
    key = jax.random.fold_in(key, 11)
    every_random_key = jax.random.split(key, 5)
    position = jnp.arange(SEQUENCE_LENGTH, dtype=jnp.float32)[None, None, :]
    position_integer = jnp.arange(SEQUENCE_LENGTH, dtype=jnp.int32)[None, None, :]
    rates = jnp.exp(jax.random.uniform(every_random_key[0], (CHANNEL_GROUP, 4, 1), jnp.float32, math.log(1.0 / (2.0 * SEQUENCE_LENGTH)), math.log(1.0 / 20.0)))
    amplitude = 0.4 * jax.random.truncated_normal(every_random_key[1], -3.0, 3.0, (CHANNEL_GROUP, 4, 1), jnp.float32)
    weights = jnp.sqrt(2.0 * rates / (1.0 - jnp.exp(-2.0 * rates * SEQUENCE_LENGTH)))
    modal = jnp.sum(amplitude * weights * jnp.exp(-rates * position), axis=1)
    spike_position = jax.random.randint(every_random_key[2], (CHANNEL_GROUP, 3, 1), 1, SEQUENCE_LENGTH)
    spike_retain_mask = jax.random.uniform(every_random_key[3], (CHANNEL_GROUP, 3, 1), jnp.float32, 0.5, 0.8)
    scale_multiplier = jnp.prod(jnp.where(position_integer >= spike_position, spike_retain_mask, 1.0), axis=1)
    rough = 0.5 * jax.random.truncated_normal(every_random_key[4], -3.0, 3.0, (CHANNEL_GROUP, SEQUENCE_LENGTH), jnp.float32) * SEQUENCE_LENGTH ** (-0.5)
    return (modal * scale_multiplier + rough).astype(jnp.float32)


def steps_of(stream_key, extent, cuts, smallest, largest):
    gain = 1.0
    for dim, shards_of in cuts:
        steps = jax.random.uniform(jax.random.fold_in(jax.random.fold_in(stream_key, 6), dim), (shards_of,), jnp.float32, smallest / len(cuts), largest / len(cuts))
        gain = gain * jnp.repeat(jnp.exp(steps), extent[dim] // shards_of).reshape((-1,) + (1,) * (len(extent) - 1 - dim))
    return gain


def bell_draw(key, extent, deviation, most, cuts=(), kind=jnp.bfloat16):
    factor_of = steps_of(key, extent, cuts, -0.22, 0.18) if cuts else 1.0
    entries = jax.random.normal(key, extent, jnp.float32) * deviation * factor_of
    return jnp.minimum(jnp.maximum(entries, -most), most).astype(kind)


def setup_inputs(seed: int = 0) -> dict:
    streams_of = jax.random.split(jax.random.key(seed), 6)
    query_gate = bell_draw(streams_of[0], (SEQS, SEQUENCE_LENGTH, CHANNEL_GROUP), 1.0, 6.0, ((0, 8), (1, 32)))
    key_gate = bell_draw(streams_of[1], (SEQS, SEQUENCE_LENGTH, CHANNEL_GROUP), 1.0, 6.0, ((0, 8), (1, 32)))
    value_in = bell_draw(streams_of[2], (SEQS, SEQUENCE_LENGTH, CHANNEL_GROUP), 1.0, 6.0, ((0, 8), (1, 32)))
    out_grad = bell_draw(streams_of[3], (SEQS, SEQUENCE_LENGTH, CHANNEL_GROUP), 1.0, 6.0, ((0, 8), (1, 32)))
    filter_taps = draw_filter_taps(jax.random.fold_in(streams_of[5], 71), 0)
    return {"query_gate": query_gate, "key_gate": key_gate, "value_in": value_in, "out_grad": out_grad, "filter_taps": filter_taps}


def spectrum(rows, padded_size):
    return jnp.fft.rfft(rows, n=padded_size, axis=-1)


def reference(query_gate, key_gate, value_in, out_grad, filter_taps):
    padded_size = 2 * SEQUENCE_LENGTH
    filter_spec = spectrum(filter_taps, padded_size)

    def one_sequence(carry, inputs):
        query_seq, key_seq, value_seq, grad_seq = inputs
        query_wide = query_seq.astype(jnp.float32)
        grad_wide = grad_seq.astype(jnp.float32)
        mixed = (key_seq.astype(jnp.float32) * value_seq.astype(jnp.float32)).astype(jnp.bfloat16)
        mixed_spec = spectrum(mixed.astype(jnp.float32).T, padded_size)
        conv_rows = jnp.fft.irfft(mixed_spec * filter_spec, n=padded_size, axis=-1)[:, :SEQUENCE_LENGTH]
        conv = conv_rows.T.astype(jnp.bfloat16)
        conv_wide = conv.astype(jnp.float32)
        mixed_out = (query_wide * conv_wide).astype(jnp.bfloat16)
        grad_mix = (grad_wide * query_wide).astype(jnp.bfloat16)
        query_grad = (grad_wide * conv_wide).astype(jnp.bfloat16)
        grad_spec = spectrum(grad_mix.astype(jnp.float32).T, padded_size)
        back_rows = jnp.fft.irfft(jnp.conj(filter_spec) * grad_spec, n=padded_size, axis=-1)[:, :SEQUENCE_LENGTH]
        back = back_rows.T.astype(jnp.bfloat16).astype(jnp.float32)
        key_grad = (back * value_seq.astype(jnp.float32)).astype(jnp.bfloat16)
        value_grad = (back * key_seq.astype(jnp.float32)).astype(jnp.bfloat16)
        filter_term = jnp.fft.irfft(jnp.conj(mixed_spec) * grad_spec, n=padded_size, axis=-1)[:, :SEQUENCE_LENGTH]
        return carry + filter_term.astype(carry.dtype), (mixed_out, query_grad, key_grad, value_grad)

    initial = jnp.zeros((CHANNEL_GROUP, SEQUENCE_LENGTH), jnp.float32)
    filter_sum, results = lax.scan(one_sequence, initial, (query_gate, key_gate, value_in, out_grad))
    mixed_out, query_grad, key_grad, value_grad = results
    filter_grad = filter_sum * (SEQUENCE_LENGTH * SEQS) ** -0.5
    return mixed_out, query_grad, key_grad, value_grad, filter_grad
```

```python
import functools
import math

import jax
import jax.numpy as jnp
import numpy as np
from jax import lax
from jax.experimental import pallas as pl
from jax.experimental.pallas import tpu as pltpu
from jax.sharding import PartitionSpec as P

MESH = pl.DeviceIdType.MESH
LANES = 128
HALF = 32
BINS = 33
GROUP = 16
CHUNK = 11
ROOT = math.sqrt(0.5)


def tables():
    step = np.arange(LANES, dtype=np.float64)
    angle = 2.0 * np.pi * ((step[:, None] * step[None, :]) % LANES) / LANES
    cos, sin = np.cos(angle), np.sin(angle)
    forward = np.block([[cos, -sin], [sin, cos]])
    inverse = np.block([[cos, sin], [-sin, cos]]) / (64.0 * LANES)
    turn = 2.0 * np.pi * (np.arange(BINS, dtype=np.float64)[:, None] * step[None, :]) / (64.0 * LANES)
    twist = np.concatenate([np.cos(turn), np.sin(turn)], axis=1)
    return (
        jnp.asarray(forward, jnp.bfloat16),
        jnp.asarray(inverse, jnp.bfloat16),
        jnp.asarray(twist, jnp.float32),
    )


def add(a, b):
    return (a[0] + b[0], a[1] + b[1])


def sub(a, b):
    return (a[0] - b[0], a[1] - b[1])


def turned(a, part):
    part = part % 1.0
    if part == 0.0:
        return a
    if part == 0.25:
        return (-a[1], a[0])
    if part == 0.5:
        return (-a[0], -a[1])
    if part == 0.75:
        return (a[1], -a[0])
    cos, sin = math.cos(2.0 * math.pi * part), math.sin(2.0 * math.pi * part)
    if part in (0.125, 0.375, 0.625, 0.875):
        c, s = math.copysign(1.0, cos), math.copysign(1.0, sin)
        real = a[0] - a[1] if c == s else a[0] + a[1]
        imag = a[0] + a[1] if c == s else a[1] - a[0]
        return ((c * ROOT) * real, (c * ROOT) * imag)
    return (a[0] * cos - a[1] * sin, a[0] * sin + a[1] * cos)


def four(x, sign):
    a, b = add(x[0], x[2]), sub(x[0], x[2])
    c, d = add(x[1], x[3]), sub(x[1], x[3])
    e = turned(d, 0.25 * sign)
    return [add(a, c), add(b, e), sub(a, c), sub(b, e)]


def eight(x, sign):
    even, odd = four(x[0::2], sign), four(x[1::2], sign)
    odd = [turned(odd[k], sign * k / 8.0) for k in range(4)]
    return [add(even[k], odd[k]) for k in range(4)] + [sub(even[k], odd[k]) for k in range(4)]


def real_eight(x):
    a, b = x[0] + x[4], x[0] - x[4]
    c, d = x[2] + x[6], x[2] - x[6]
    e, f = x[1] + x[5], x[1] - x[5]
    g, h = x[3] + x[7], x[3] - x[7]
    p, q = ROOT * (f - h), ROOT * (f + h)
    return [
        (a + c) + (e + g),
        (b + p, -d - q),
        (a - c, g - e),
        (b - p, d - q),
        (a + c) - (e + g),
    ]


def block_forward(x):
    cols = [[] for _ in range(5)]
    for b in range(8):
        x0, x1, x2, x3 = x[b], x[8 + b], x[16 + b], x[24 + b]
        p, q = x0 + x2, x1 + x3
        m, n = ROOT * (x1 - x3), ROOT * q
        cols[0].append(p + q)
        cols[1].append(turned((x0 + m, -x2 - n), -b / 64.0))
        cols[2].append(turned((x0 - x2, x3 - x1), -2 * b / 64.0))
        cols[3].append(turned((x0 - m, x2 - n), -3 * b / 64.0))
        cols[4].append(p - q)
    out = [None] * BINS
    for d, value in enumerate(real_eight(cols[0])):
        out[8 * d] = value
    for c in (1, 2, 3):
        for d, value in enumerate(eight(cols[c], -1)):
            k = c + 8 * d
            if k <= 32:
                out[k] = value
            else:
                out[64 - k] = (value[0], -value[1])
    r = cols[4]
    u = four([turned((r[b], -r[b + 4]), -b / 16.0) for b in range(4)], -1)
    out[4], out[20] = u[0], u[1]
    out[28] = (u[2][0], -u[2][1])
    out[12] = (u[3][0], -u[3][1])
    return out


def real_back(t0, t1, t2, t3, t4, count):
    a, b = t0 + t4, t0 - t4
    r2, i2 = 2.0 * t2[0], 2.0 * t2[1]
    even = [a + r2, b - i2, a - r2, b + i2]
    odd = [
        2.0 * (t1[0] + t3[0]),
        (2.0 * ROOT) * ((t1[0] - t1[1]) - (t3[0] + t3[1])),
        2.0 * (t3[1] - t1[1]),
        (2.0 * ROOT) * ((t3[0] - t3[1]) - (t1[0] + t1[1])),
    ]
    first = [even[k] + odd[k] for k in range(4)]
    if count == 4:
        return first
    return first + [even[k] - odd[k] for k in range(4)]


def block_inverse(v):
    t = [None] * 5
    t[0] = real_back(v[0], v[8], v[16], v[24], v[32], 8)
    for c in (1, 2, 3):
        u = []
        for d in range(8):
            k = c + 8 * d
            u.append(v[k] if k <= 32 else (v[64 - k][0], -v[64 - k][1]))
        u = eight(u, 1)
        t[c] = [turned(u[b], b * c / 64.0) for b in range(8)]
    g = four([v[4], v[20], (v[28][0], -v[28][1]), (v[12][0], -v[12][1])], 1)
    g = [turned(g[b], b / 16.0) for b in range(4)]
    t[4] = [2.0 * g[b][0] for b in range(4)] + [-2.0 * g[b][1] for b in range(4)]
    out = [None] * HALF
    for b in range(8):
        for a, value in enumerate(real_back(t[0][b], t[1][b], t[2][b], t[3][b], t[4][b], 4)):
            out[8 * a + b] = value
    return out


def analyse(read, twist, packed, channels):
    def body(g, carry):
        rows = pl.ds(pl.multiple_of(g * GROUP, GROUP), GROUP)
        bins = block_forward([read(j, rows) for j in range(HALF)])
        for k in range(BINS):
            if k == 0:
                real, imag = bins[0], jnp.zeros_like(bins[0])
            else:
                cos, sin = twist[k : k + 1, :LANES], twist[k : k + 1, LANES:]
                if k == 32:
                    real, imag = bins[k] * cos, -(bins[k] * sin)
                else:
                    real = bins[k][0] * cos + bins[k][1] * sin
                    imag = bins[k][1] * cos - bins[k][0] * sin
            packed[k, rows, :LANES] = real.astype(jnp.bfloat16)
            packed[k, rows, LANES:] = imag.astype(jnp.bfloat16)
        return carry

    lax.fori_loop(0, channels // GROUP, body, 0)


def synthesise(wide, twist, write, channels):
    def body(g, carry):
        rows = pl.ds(pl.multiple_of(g * GROUP, GROUP), GROUP)
        bins = []
        for k in range(BINS):
            real, imag = wide[k, rows, :LANES], wide[k, rows, LANES:]
            cos, sin = twist[k : k + 1, :LANES], twist[k : k + 1, LANES:]
            if k == 0:
                bins.append(real)
            elif k == 32:
                bins.append(real * cos - imag * sin)
            else:
                bins.append((real * cos - imag * sin, real * sin + imag * cos))
        for j, value in enumerate(block_inverse(bins)):
            write(j, rows, value)
        return carry

    lax.fori_loop(0, channels // GROUP, body, 0)


def chunks(body):
    def step(i, carry):
        body(pl.ds(i * CHUNK, CHUNK))
        return carry

    lax.fori_loop(0, BINS // CHUNK, step, 0)


def times(rows, matrix):
    flat = rows.reshape(-1, 2 * LANES)
    out = jnp.dot(flat, matrix, preferred_element_type=jnp.float32)
    return out.reshape(rows.shape)


def times_conj(a, b):
    ar, ai, br, bi = a[..., :LANES], a[..., LANES:], b[..., :LANES], b[..., LANES:]
    return jnp.concatenate([ar * br + ai * bi, ar * bi - ai * br], axis=-1)


def times_plain(a, b):
    ar, ai, br, bi = a[..., :LANES], a[..., LANES:], b[..., :LANES], b[..., LANES:]
    return jnp.concatenate([ar * br - ai * bi, ar * bi + ai * br], axis=-1)


def mixing(
    peers,
    query,
    key,
    value,
    grad,
    taps_in,
    forward_in,
    inverse_in,
    twist_in,
    conv_out,
    back_out,
    filter_out,
    gate,
    taps,
    forward,
    inverse,
    twist,
    sent,
    got,
    replied,
    answer,
    packed,
    wide,
    filter_spec,
    mixed_spec,
    grad_spec,
    term,
    term_got,
    half,
    half_got,
    load_sem,
    send_sem,
    recv_sem,
    term_sem,
    half_sem,
    store_sem,
):
    me = lax.axis_index("ctx")
    dp = lax.axis_index("dp")
    line, side = dp // 2, dp % 2
    channels = taps.shape[0]
    chunk_rows = sent.shape[2]

    barrier = pltpu.get_barrier_semaphore()

    def greet(i, carry):
        pl.semaphore_signal(
            barrier, inc=1, device_id={"ctx": lax.rem(me + i, peers)}, device_id_type=MESH
        )
        return carry

    lax.fori_loop(1, peers, greet, 0)
    for i in range(1, 4):
        pl.semaphore_signal(
            barrier, inc=1, device_id={"dp": lax.rem(line + i, 4) * 2 + side}, device_id_type=MESH
        )
    pl.semaphore_signal(barrier, inc=1, device_id={"dp": line * 2 + 1 - side}, device_id_type=MESH)

    loads = [
        pltpu.make_async_copy(source, target, load_sem.at[n])
        for n, (source, target) in enumerate(
            [
                (key, gate.at[0]),
                (value, gate.at[1]),
                (query, gate.at[2]),
                (grad, gate.at[3]),
                (taps_in, taps),
                (forward_in, forward),
                (inverse_in, inverse),
                (twist_in, twist),
            ]
        )
    ]
    for load in loads:
        load.start()

    def gated(first, second, slot):
        def body(t, carry):
            lanes = pl.ds(pl.multiple_of(t * LANES, LANES), LANES)
            product = gate[first, :, lanes].astype(jnp.float32) * gate[second, :, lanes].astype(jnp.float32)
            flipped = jnp.transpose(product).astype(jnp.bfloat16)
            sent[slot, pl.ds(2 * t, 2)] = flipped.reshape(2, LANES // 2, LANES)
            return carry

        lax.fori_loop(0, peers // 2, body, 0)
        got[slot, me] = sent[slot, me]

    def scatter(source, target, slot, sem_base):
        def body(i, carry):
            peer = lax.rem(me + i, peers)
            pltpu.make_async_remote_copy(
                src_ref=source.at[slot, peer],
                dst_ref=target.at[slot, me],
                send_sem=send_sem.at[sem_base + slot],
                recv_sem=recv_sem.at[sem_base + slot],
                device_id={"ctx": peer},
                device_id_type=MESH,
            ).start()
            return carry

        lax.fori_loop(1, peers, body, 0)

    def whole(source, target, slot, sem_base):
        part = pl.ds(0, peers - 1)
        return pltpu.make_async_remote_copy(
            src_ref=source.at[slot, part],
            dst_ref=target.at[slot, part],
            send_sem=send_sem.at[sem_base + slot],
            recv_sem=recv_sem.at[sem_base + slot],
            device_id={"ctx": lax.rem(me + 1, peers)},
            device_id_type=MESH,
        )

    loads[0].wait()
    loads[1].wait()
    gated(0, 1, 0)
    pl.semaphore_wait(barrier, peers - 1 + 4)
    scatter(sent, got, 0, 0)
    loads[2].wait()
    loads[3].wait()
    gated(2, 3, 1)
    scatter(sent, got, 1, 0)
    for load in loads[4:]:
        load.wait()

    analyse(lambda j, rows: taps[rows, j * LANES : (j + 1) * LANES], twist, packed, channels)

    def filter_step(k):
        filter_spec[k] = times(packed[k], forward[...])

    chunks(filter_step)

    def convolve(slot, spectrum, product):
        whole(sent, got, slot, 0).wait_recv()
        analyse(lambda j, rows: got[slot, j, rows, :].astype(jnp.float32), twist, packed, channels)

        def step(k):
            spec = times(packed[k], forward[...])
            spectrum[k] = spec
            wide[k] = times(product(filter_spec[k], spec).astype(jnp.bfloat16), inverse[...])

        chunks(step)

        def write(j, rows, values):
            replied[slot, j, rows, :] = values.astype(jnp.bfloat16)

        synthesise(wide, twist, write, channels)
        answer[slot, me] = replied[slot, me]
        scatter(replied, answer, slot, 2)

    convolve(0, mixed_spec, times_plain)
    convolve(1, grad_spec, times_conj)

    def term_step(k):
        wide[k] = times(times_conj(mixed_spec[k], grad_spec[k]).astype(jnp.bfloat16), inverse[...])

    chunks(term_step)

    def write_term(j, rows, values):
        term[j, rows, :] = values.astype(jnp.bfloat16)

    synthesise(wide, twist, write_term, channels)

    hops = []
    for i in range(1, 4):
        other = lax.rem(line + i, 4)
        hops.append(
            pltpu.make_async_remote_copy(
                src_ref=term.at[pl.ds(other * 8, 8)],
                dst_ref=term_got.at[i - 1],
                send_sem=term_sem.at[i - 1],
                recv_sem=term_sem.at[i + 2],
                device_id={"dp": other * 2 + side},
                device_id_type=MESH,
            )
        )
    for hop in hops:
        hop.start()
    for hop in hops:
        hop.wait_recv()

    def total(which):
        mine = term[pl.ds(line * 8 + which * 4, 4)].astype(jnp.float32)
        for i in range(3):
            mine += term_got[i, pl.ds(which * 4, 4)].astype(jnp.float32)
        return mine

    half[...] = total(1 - side).astype(jnp.bfloat16)
    cross = pltpu.make_async_remote_copy(
        src_ref=half,
        dst_ref=half_got,
        send_sem=half_sem.at[0],
        recv_sem=half_sem.at[1],
        device_id={"dp": line * 2 + 1 - side},
        device_id_type=MESH,
    )
    cross.start()
    kept = total(side)
    cross.wait_recv()
    kept += half_got[...].astype(jnp.float32)
    for j in range(4):
        filter_out[:, j * LANES : (j + 1) * LANES] = kept[j]

    whole(replied, answer, 0, 2).wait_recv()
    conv_store = pltpu.make_async_copy(answer.at[0], conv_out, store_sem.at[0])
    conv_store.start()
    whole(replied, answer, 1, 2).wait_recv()
    back_store = pltpu.make_async_copy(answer.at[1], back_out, store_sem.at[1])
    back_store.start()
    for slot in range(2):
        whole(sent, got, slot, 0).wait_send()
        whole(replied, answer, slot, 2).wait_send()
    for hop in hops:
        hop.wait_send()
    cross.wait_send()
    conv_store.wait()
    back_store.wait()


def finish(scale, query, key, value, grad, conv, back, total, mixed_out, query_grad, key_grad, value_grad, filter_grad):
    def tokens(ref):
        rows = ref[...].reshape(-1, LANES).astype(jnp.float32)
        return jnp.transpose(rows)

    conv_wide = tokens(conv)
    mixed_out[0] = (query[0].astype(jnp.float32) * conv_wide).astype(jnp.bfloat16)
    query_grad[0] = (grad[0].astype(jnp.float32) * conv_wide).astype(jnp.bfloat16)
    back_wide = tokens(back)
    key_grad[0] = (back_wide * value[0].astype(jnp.float32)).astype(jnp.bfloat16)
    value_grad[0] = (back_wide * key[0].astype(jnp.float32)).astype(jnp.bfloat16)
    filter_grad[...] = total[...] * scale


def shards(query_gate, key_gate, value_in, out_grad, filter_taps):
    _, block, width = query_gate.shape
    channels, seq_len = filter_taps.shape
    peers = lax.axis_size("ctx")
    parts = lax.axis_size("dp")
    forward, inverse, twist = tables()
    anywhere = pl.BlockSpec(memory_space=pl.ANY)
    in_vmem = pl.BlockSpec(memory_space=pltpu.VMEM)
    planes = (peers, channels, LANES)
    spectrum = pltpu.VMEM((BINS, channels, 2 * LANES), jnp.float32)
    share = seq_len // parts
    conv, back, total = pl.pallas_call(
        functools.partial(mixing, peers),
        out_shape=(
            jax.ShapeDtypeStruct(planes, jnp.bfloat16),
            jax.ShapeDtypeStruct(planes, jnp.bfloat16),
            jax.ShapeDtypeStruct((channels, share), jnp.float32),
        ),
        in_specs=[anywhere] * 8,
        out_specs=(anywhere, anywhere, in_vmem),
        scratch_shapes=[
            pltpu.VMEM((4, block, width), jnp.bfloat16),
            pltpu.VMEM((channels, seq_len), jnp.float32),
            pltpu.VMEM((2 * LANES, 2 * LANES), jnp.bfloat16),
            pltpu.VMEM((2 * LANES, 2 * LANES), jnp.bfloat16),
            pltpu.VMEM((BINS, 2 * LANES), jnp.float32),
            pltpu.VMEM((2,) + planes, jnp.bfloat16),
            pltpu.VMEM((2,) + planes, jnp.bfloat16),
            pltpu.VMEM((2,) + planes, jnp.bfloat16),
            pltpu.VMEM((2,) + planes, jnp.bfloat16),
            pltpu.VMEM((BINS, channels, 2 * LANES), jnp.bfloat16),
            spectrum,
            spectrum,
            spectrum,
            spectrum,
            pltpu.VMEM(planes, jnp.bfloat16),
            pltpu.VMEM((3, 8, channels, LANES), jnp.bfloat16),
            pltpu.VMEM((4, channels, LANES), jnp.bfloat16),
            pltpu.VMEM((4, channels, LANES), jnp.bfloat16),
            pltpu.SemaphoreType.DMA((8,)),
            pltpu.SemaphoreType.DMA((4,)),
            pltpu.SemaphoreType.DMA((4,)),
            pltpu.SemaphoreType.DMA((6,)),
            pltpu.SemaphoreType.DMA((2,)),
            pltpu.SemaphoreType.DMA((2,)),
        ],
        compiler_params=pltpu.CompilerParams(
            collective_id=0, has_side_effects=True, vmem_limit_bytes=48 << 20
        ),
        name="mixing",
    )(
        query_gate[0],
        key_gate[0],
        value_in[0],
        out_grad[0],
        filter_taps,
        forward,
        inverse,
        twist,
    )

    steps = 8
    wide = width // steps
    token_spec = pl.BlockSpec((1, block, wide), lambda t: (0, 0, t))
    plane_spec = pl.BlockSpec((peers // steps, channels, LANES), lambda t: (t, 0, 0))
    filter_block = pl.BlockSpec((channels // steps, share), lambda t: (t, 0))
    tokens = jax.ShapeDtypeStruct(query_gate.shape, jnp.bfloat16)
    return pl.pallas_call(
        functools.partial(finish, (seq_len * parts) ** (-0.5)),
        grid=(steps,),
        out_shape=(tokens,) * 4 + (jax.ShapeDtypeStruct((channels, share), jnp.float32),),
        in_specs=[token_spec] * 4 + [plane_spec] * 2 + [filter_block],
        out_specs=(token_spec,) * 4 + (filter_block,),
        name="finish",
    )(query_gate, key_gate, value_in, out_grad, conv, back, total)


def solution(mesh):
    placed = (
        P("dp", "ctx", None),
        P("dp", "ctx", None),
        P("dp", "ctx", None),
        P("dp", "ctx", None),
        P("ctx", None),
    )
    return jax.shard_map(
        shards,
        mesh=mesh,
        in_specs=placed,
        out_specs=(
            P("dp", "ctx", None),
            P("dp", "ctx", None),
            P("dp", "ctx", None),
            P("dp", "ctx", None),
            P("ctx", "dp"),
        ),
        check_vma=False,
    )
```

```python
import functools
import math

import jax
import jax.numpy as jnp
import numpy as np
from jax import lax
from jax.experimental import pallas as pl
from jax.experimental.pallas import tpu as pltpu
from jax.sharding import PartitionSpec as P

MESH = pl.DeviceIdType.MESH
LANES = 128
HALF = 32
BINS = 33
GROUP = 16
CHUNK = 11
ROOT = math.sqrt(0.5)


def tables():
    step = np.arange(LANES, dtype=np.float64)
    angle = 2.0 * np.pi * ((step[:, None] * step[None, :]) % LANES) / LANES
    cos, sin = np.cos(angle), np.sin(angle)
    forward = np.block([[cos, -sin], [sin, cos]])
    inverse = np.block([[cos, sin], [-sin, cos]]) / (64.0 * LANES)
    turn = 2.0 * np.pi * (np.arange(BINS, dtype=np.float64)[:, None] * step[None, :]) / (64.0 * LANES)
    twist = np.concatenate([np.cos(turn), np.sin(turn)], axis=1)
    return (
        jnp.asarray(forward, jnp.bfloat16),
        jnp.asarray(inverse, jnp.bfloat16),
        jnp.asarray(twist, jnp.float32),
    )


def add(a, b):
    return (a[0] + b[0], a[1] + b[1])


def sub(a, b):
    return (a[0] - b[0], a[1] - b[1])


def turned(a, part):
    part = part % 1.0
    if part == 0.0:
        return a
    if part == 0.25:
        return (-a[1], a[0])
    if part == 0.5:
        return (-a[0], -a[1])
    if part == 0.75:
        return (a[1], -a[0])
    cos, sin = math.cos(2.0 * math.pi * part), math.sin(2.0 * math.pi * part)
    if part in (0.125, 0.375, 0.625, 0.875):
        c, s = math.copysign(1.0, cos), math.copysign(1.0, sin)
        real = a[0] - a[1] if c == s else a[0] + a[1]
        imag = a[0] + a[1] if c == s else a[1] - a[0]
        return ((c * ROOT) * real, (c * ROOT) * imag)
    return (a[0] * cos - a[1] * sin, a[0] * sin + a[1] * cos)


def four(x, sign):
    a, b = add(x[0], x[2]), sub(x[0], x[2])
    c, d = add(x[1], x[3]), sub(x[1], x[3])
    e = turned(d, 0.25 * sign)
    return [add(a, c), add(b, e), sub(a, c), sub(b, e)]


def eight(x, sign):
    even, odd = four(x[0::2], sign), four(x[1::2], sign)
    odd = [turned(odd[k], sign * k / 8.0) for k in range(4)]
    return [add(even[k], odd[k]) for k in range(4)] + [sub(even[k], odd[k]) for k in range(4)]


def real_eight(x):
    a, b = x[0] + x[4], x[0] - x[4]
    c, d = x[2] + x[6], x[2] - x[6]
    e, f = x[1] + x[5], x[1] - x[5]
    g, h = x[3] + x[7], x[3] - x[7]
    p, q = ROOT * (f - h), ROOT * (f + h)
    return [
        (a + c) + (e + g),
        (b + p, -d - q),
        (a - c, g - e),
        (b - p, d - q),
        (a + c) - (e + g),
    ]


def block_forward(x):
    cols = [[] for _ in range(5)]
    for b in range(8):
        x0, x1, x2, x3 = x[b], x[8 + b], x[16 + b], x[24 + b]
        p, q = x0 + x2, x1 + x3
        m, n = ROOT * (x1 - x3), ROOT * q
        cols[0].append(p + q)
        cols[1].append(turned((x0 + m, -x2 - n), -b / 64.0))
        cols[2].append(turned((x0 - x2, x3 - x1), -2 * b / 64.0))
        cols[3].append(turned((x0 - m, x2 - n), -3 * b / 64.0))
        cols[4].append(p - q)
    out = [None] * BINS
    for d, value in enumerate(real_eight(cols[0])):
        out[8 * d] = value
    for c in (1, 2, 3):
        for d, value in enumerate(eight(cols[c], -1)):
            k = c + 8 * d
            if k <= 32:
                out[k] = value
            else:
                out[64 - k] = (value[0], -value[1])
    r = cols[4]
    u = four([turned((r[b], -r[b + 4]), -b / 16.0) for b in range(4)], -1)
    out[4], out[20] = u[0], u[1]
    out[28] = (u[2][0], -u[2][1])
    out[12] = (u[3][0], -u[3][1])
    return out


def real_back(t0, t1, t2, t3, t4, count):
    a, b = t0 + t4, t0 - t4
    r2, i2 = 2.0 * t2[0], 2.0 * t2[1]
    even = [a + r2, b - i2, a - r2, b + i2]
    odd = [
        2.0 * (t1[0] + t3[0]),
        (2.0 * ROOT) * ((t1[0] - t1[1]) - (t3[0] + t3[1])),
        2.0 * (t3[1] - t1[1]),
        (2.0 * ROOT) * ((t3[0] - t3[1]) - (t1[0] + t1[1])),
    ]
    first = [even[k] + odd[k] for k in range(4)]
    if count == 4:
        return first
    return first + [even[k] - odd[k] for k in range(4)]


def block_inverse(v):
    t = [None] * 5
    t[0] = real_back(v[0], v[8], v[16], v[24], v[32], 8)
    for c in (1, 2, 3):
        u = []
        for d in range(8):
            k = c + 8 * d
            u.append(v[k] if k <= 32 else (v[64 - k][0], -v[64 - k][1]))
        u = eight(u, 1)
        t[c] = [turned(u[b], b * c / 64.0) for b in range(8)]
    g = four([v[4], v[20], (v[28][0], -v[28][1]), (v[12][0], -v[12][1])], 1)
    g = [turned(g[b], b / 16.0) for b in range(4)]
    t[4] = [2.0 * g[b][0] for b in range(4)] + [-2.0 * g[b][1] for b in range(4)]
    out = [None] * HALF
    for b in range(8):
        for a, value in enumerate(real_back(t[0][b], t[1][b], t[2][b], t[3][b], t[4][b], 4)):
            out[8 * a + b] = value
    return out


def analyse(read, twist, packed, channels):
    def body(g, carry):
        rows = pl.ds(pl.multiple_of(g * GROUP, GROUP), GROUP)
        bins = block_forward([read(j, rows) for j in range(HALF)])
        for k in range(BINS):
            if k == 0:
                real, imag = bins[0], jnp.zeros_like(bins[0])
            else:
                cos, sin = twist[k : k + 1, :LANES], twist[k : k + 1, LANES:]
                if k == 32:
                    real, imag = bins[k] * cos, -(bins[k] * sin)
                else:
                    real = bins[k][0] * cos + bins[k][1] * sin
                    imag = bins[k][1] * cos - bins[k][0] * sin
            packed[k, rows, :LANES] = real.astype(jnp.bfloat16)
            packed[k, rows, LANES:] = imag.astype(jnp.bfloat16)
        return carry

    lax.fori_loop(0, channels // GROUP, body, 0)


def synthesise(wide, twist, write, channels):
    def body(g, carry):
        rows = pl.ds(pl.multiple_of(g * GROUP, GROUP), GROUP)
        bins = []
        for k in range(BINS):
            real, imag = wide[k, rows, :LANES], wide[k, rows, LANES:]
            cos, sin = twist[k : k + 1, :LANES], twist[k : k + 1, LANES:]
            if k == 0:
                bins.append(real)
            elif k == 32:
                bins.append(real * cos - imag * sin)
            else:
                bins.append((real * cos - imag * sin, real * sin + imag * cos))
        for j, value in enumerate(block_inverse(bins)):
            write(j, rows, value)
        return carry

    lax.fori_loop(0, channels // GROUP, body, 0)


def chunks(body):
    def step(i, carry):
        body(pl.ds(i * CHUNK, CHUNK))
        return carry

    lax.fori_loop(0, BINS // CHUNK, step, 0)


def times(rows, matrix):
    flat = rows.reshape(-1, 2 * LANES)
    out = jnp.dot(flat, matrix, preferred_element_type=jnp.float32)
    return out.reshape(rows.shape)


def times_conj(a, b):
    ar, ai, br, bi = a[..., :LANES], a[..., LANES:], b[..., :LANES], b[..., LANES:]
    return jnp.concatenate([ar * br + ai * bi, ar * bi - ai * br], axis=-1)


def times_plain(a, b):
    ar, ai, br, bi = a[..., :LANES], a[..., LANES:], b[..., :LANES], b[..., LANES:]
    return jnp.concatenate([ar * br - ai * bi, ar * bi + ai * br], axis=-1)


def mixing(
    peers,
    scale,
    query,
    key,
    value,
    grad,
    taps_in,
    forward_in,
    inverse_in,
    twist_in,
    mixed_out,
    query_grad,
    key_grad,
    value_grad,
    filter_out,
    gate,
    taps,
    forward,
    inverse,
    twist,
    sent,
    got,
    replied,
    answer,
    packed,
    wide,
    filter_spec,
    mixed_spec,
    grad_spec,
    term,
    term_got,
    half,
    half_got,
    load_sem,
    send_sem,
    recv_sem,
    term_sem,
    half_sem,
    back_sem,
):
    me = lax.axis_index("ctx")
    dp = lax.axis_index("dp")
    line, side = dp // 2, dp % 2
    channels = taps.shape[0]

    barrier = pltpu.get_barrier_semaphore()

    def greet(i, carry):
        pl.semaphore_signal(
            barrier, inc=1, device_id={"ctx": lax.rem(me + i, peers)}, device_id_type=MESH
        )
        return carry

    lax.fori_loop(1, peers, greet, 0)
    for i in range(1, 4):
        pl.semaphore_signal(
            barrier, inc=1, device_id={"dp": lax.rem(line + i, 4) * 2 + side}, device_id_type=MESH
        )
    pl.semaphore_signal(barrier, inc=1, device_id={"dp": line * 2 + 1 - side}, device_id_type=MESH)

    loads = [
        pltpu.make_async_copy(source, target, load_sem.at[n])
        for n, (source, target) in enumerate(
            [
                (key, gate.at[0]),
                (value, gate.at[1]),
                (query, gate.at[2]),
                (grad, gate.at[3]),
                (taps_in, taps),
                (forward_in, forward),
                (inverse_in, inverse),
                (twist_in, twist),
            ]
        )
    ]
    for load in loads:
        load.start()

    def gated(first, second, slot):
        def body(t, carry):
            lanes = pl.ds(pl.multiple_of(t * LANES, LANES), LANES)
            product = gate[first, :, lanes].astype(jnp.float32) * gate[second, :, lanes].astype(jnp.float32)
            flipped = jnp.transpose(product).astype(jnp.bfloat16)
            sent[slot, pl.ds(2 * t, 2)] = flipped.reshape(2, LANES // 2, LANES)
            return carry

        lax.fori_loop(0, peers // 2, body, 0)
        got[slot, me] = sent[slot, me]

    def scatter(source, target, slot, sem_base):
        def body(i, carry):
            peer = lax.rem(me + i, peers)
            last = sem_base + slot == 3
            pltpu.make_async_remote_copy(
                src_ref=source.at[slot, peer],
                dst_ref=target.at[slot, me],
                send_sem=send_sem.at[sem_base + slot],
                recv_sem=back_sem.at[me] if last else recv_sem.at[sem_base + slot],
                device_id={"ctx": peer},
                device_id_type=MESH,
            ).start()
            return carry

        lax.fori_loop(1, peers, body, 0)

    def whole(source, target, slot, sem_base):
        part = pl.ds(0, peers - 1)
        return pltpu.make_async_remote_copy(
            src_ref=source.at[slot, part],
            dst_ref=target.at[slot, part],
            send_sem=send_sem.at[sem_base + slot],
            recv_sem=recv_sem.at[sem_base + slot],
            device_id={"ctx": lax.rem(me + 1, peers)},
            device_id_type=MESH,
        )

    loads[0].wait()
    loads[1].wait()
    gated(0, 1, 0)
    pl.semaphore_wait(barrier, peers - 1 + 4)
    scatter(sent, got, 0, 0)
    loads[2].wait()
    loads[3].wait()
    gated(2, 3, 1)
    scatter(sent, got, 1, 0)
    for load in loads[4:]:
        load.wait()

    analyse(lambda j, rows: taps[rows, j * LANES : (j + 1) * LANES], twist, packed, channels)

    def filter_step(k):
        filter_spec[k] = times(packed[k], forward[...])

    chunks(filter_step)

    def convolve(slot, spectrum, product):
        whole(sent, got, slot, 0).wait_recv()
        analyse(lambda j, rows: got[slot, j, rows, :].astype(jnp.float32), twist, packed, channels)

        def step(k):
            spec = times(packed[k], forward[...])
            spectrum[k] = spec
            wide[k] = times(product(filter_spec[k], spec).astype(jnp.bfloat16), inverse[...])

        chunks(step)

        def write(j, rows, values):
            replied[slot, j, rows, :] = values.astype(jnp.bfloat16)

        synthesise(wide, twist, write, channels)
        answer[slot, me] = replied[slot, me]
        scatter(replied, answer, slot, 2)

    convolve(0, mixed_spec, times_plain)
    convolve(1, grad_spec, times_conj)

    def term_step(k):
        wide[k] = times(times_conj(mixed_spec[k], grad_spec[k]).astype(jnp.bfloat16), inverse[...])

    chunks(term_step)

    def write_term(j, rows, values):
        term[j, rows, :] = values.astype(jnp.bfloat16)

    synthesise(wide, twist, write_term, channels)

    hops = []
    for i in range(1, 4):
        other = lax.rem(line + i, 4)
        hops.append(
            pltpu.make_async_remote_copy(
                src_ref=term.at[pl.ds(other * 8, 8)],
                dst_ref=term_got.at[i - 1],
                send_sem=term_sem.at[i - 1],
                recv_sem=term_sem.at[i + 2],
                device_id={"dp": other * 2 + side},
                device_id_type=MESH,
            )
        )
    for hop in hops:
        hop.start()
    for hop in hops:
        hop.wait_recv()

    def total(which):
        mine = term[pl.ds(line * 8 + which * 4, 4)].astype(jnp.float32)
        for i in range(3):
            mine += term_got[i, pl.ds(which * 4, 4)].astype(jnp.float32)
        return mine

    half[...] = total(1 - side).astype(jnp.bfloat16)
    cross = pltpu.make_async_remote_copy(
        src_ref=half,
        dst_ref=half_got,
        send_sem=half_sem.at[0],
        recv_sem=half_sem.at[1],
        device_id={"dp": line * 2 + 1 - side},
        device_id_type=MESH,
    )
    cross.start()
    kept = total(side)
    cross.wait_recv()
    kept += half_got[...].astype(jnp.float32)
    for j in range(4):
        filter_out[:, j * LANES : (j + 1) * LANES] = kept[j] * scale

    def tile(slot, t, first, second, first_out, second_out):
        lanes = pl.ds(pl.multiple_of(t * LANES, LANES), LANES)
        rows = answer[slot, pl.ds(2 * t, 2)].reshape(LANES, LANES)
        wide_rows = jnp.transpose(rows.astype(jnp.float32))
        first_out[0, :, lanes] = (gate[first, :, lanes].astype(jnp.float32) * wide_rows).astype(jnp.bfloat16)
        second_out[0, :, lanes] = (gate[second, :, lanes].astype(jnp.float32) * wide_rows).astype(jnp.bfloat16)

    whole(replied, answer, 0, 2).wait_recv()

    def conv_tile(t, carry):
        tile(0, t, 2, 3, mixed_out, query_grad)
        return carry

    lax.fori_loop(0, peers // 2, conv_tile, 0)

    def back_tile(i, carry):
        t = lax.rem(me // 2 + peers // 2 - i, peers // 2)
        for source in (2 * t, 2 * t + 1):

            @pl.when(source != me)
            def _():
                pltpu.make_async_remote_copy(
                    src_ref=replied.at[1, source],
                    dst_ref=answer.at[1, source],
                    send_sem=send_sem.at[3],
                    recv_sem=back_sem.at[source],
                    device_id={"ctx": lax.rem(me + 1, peers)},
                    device_id_type=MESH,
                ).wait_recv()

        tile(1, t, 1, 0, key_grad, value_grad)
        return carry

    lax.fori_loop(0, peers // 2, back_tile, 0)
    for slot in range(2):
        whole(sent, got, slot, 0).wait_send()
        whole(replied, answer, slot, 2).wait_send()
    for hop in hops:
        hop.wait_send()
    cross.wait_send()


def finish(*refs):
    held, out, sem = refs[:5], refs[5:10], refs[10]
    copies = [pltpu.make_async_copy(a, b, sem.at[n]) for n, (a, b) in enumerate(zip(held, out))]
    for copy in copies:
        copy.start()
    for copy in copies:
        copy.wait()


def shards(query_gate, key_gate, value_in, out_grad, filter_taps):
    _, block, width = query_gate.shape
    channels, seq_len = filter_taps.shape
    peers = lax.axis_size("ctx")
    parts = lax.axis_size("dp")
    forward, inverse, twist = tables()
    in_hbm = pl.BlockSpec(memory_space=pltpu.HBM)
    in_vmem = pl.BlockSpec(memory_space=pltpu.VMEM)
    planes = (peers, channels, LANES)
    spectrum = pltpu.VMEM((BINS, channels, 2 * LANES), jnp.float32)
    share = seq_len // parts
    tokens = jax.ShapeDtypeStruct(query_gate.shape, jnp.bfloat16)
    shapes = (tokens,) * 4 + (jax.ShapeDtypeStruct((channels, share), jnp.float32),)
    held = pl.pallas_call(
        functools.partial(mixing, peers, (seq_len * parts) ** (-0.5)),
        out_shape=tuple(pltpu.VMEM(a.shape, a.dtype) for a in shapes),
        in_specs=[in_hbm] * 8,
        out_specs=(in_vmem,) * 5,
        scratch_shapes=[
            pltpu.VMEM((4, block, width), jnp.bfloat16),
            pltpu.VMEM((channels, seq_len), jnp.float32),
            pltpu.VMEM((2 * LANES, 2 * LANES), jnp.bfloat16),
            pltpu.VMEM((2 * LANES, 2 * LANES), jnp.bfloat16),
            pltpu.VMEM((BINS, 2 * LANES), jnp.float32),
            pltpu.VMEM((2,) + planes, jnp.bfloat16),
            pltpu.VMEM((2,) + planes, jnp.bfloat16),
            pltpu.VMEM((2,) + planes, jnp.bfloat16),
            pltpu.VMEM((2,) + planes, jnp.bfloat16),
            pltpu.VMEM((BINS, channels, 2 * LANES), jnp.bfloat16),
            spectrum,
            spectrum,
            spectrum,
            spectrum,
            pltpu.VMEM(planes, jnp.bfloat16),
            pltpu.VMEM((3, 8, channels, LANES), jnp.bfloat16),
            pltpu.VMEM((4, channels, LANES), jnp.bfloat16),
            pltpu.VMEM((4, channels, LANES), jnp.bfloat16),
            pltpu.SemaphoreType.DMA((8,)),
            pltpu.SemaphoreType.DMA((4,)),
            pltpu.SemaphoreType.DMA((4,)),
            pltpu.SemaphoreType.DMA((6,)),
            pltpu.SemaphoreType.DMA((2,)),
            pltpu.SemaphoreType.DMA((peers,)),
        ],
        compiler_params=pltpu.CompilerParams(
            collective_id=0, has_side_effects=True, vmem_limit_bytes=32 << 20
        ),
        name="mixing",
    )(
        *(
            pltpu.with_memory_space_constraint(a, pltpu.HBM)
            for a in (
                query_gate[0],
                key_gate[0],
                value_in[0],
                out_grad[0],
                filter_taps,
                forward,
                inverse,
                twist,
            )
        )
    )

    return pl.pallas_call(
        finish,
        out_shape=tuple(pltpu.HBM(a.shape, a.dtype) for a in shapes),
        in_specs=[in_vmem] * 5,
        out_specs=(in_hbm,) * 5,
        scratch_shapes=[pltpu.SemaphoreType.DMA((5,))],
        name="finish",
    )(*(pltpu.with_memory_space_constraint(a, pltpu.VMEM) for a in held))


def solution(mesh):
    placed = (
        P("dp", "ctx", None),
        P("dp", "ctx", None),
        P("dp", "ctx", None),
        P("dp", "ctx", None),
        P("ctx", None),
    )
    return jax.shard_map(
        shards,
        mesh=mesh,
        in_specs=placed,
        out_specs=(
            P("dp", "ctx", None),
            P("dp", "ctx", None),
            P("dp", "ctx", None),
            P("dp", "ctx", None),
            P("ctx", "dp"),
        ),
        check_vma=False,
    )
```

```python
import functools
import math

import jax
import jax.numpy as jnp
import numpy as np
from jax import lax
from jax.experimental import pallas as pl
from jax.experimental.pallas import tpu as pltpu
from jax.sharding import PartitionSpec as P

MESH = pl.DeviceIdType.MESH
LANES = 128
HALF = 32
BINS = 33
GROUP = 16
CHUNK = 11
PIECES = 2
ROOT = math.sqrt(0.5)


def tables():
    step = np.arange(LANES, dtype=np.float64)
    angle = 2.0 * np.pi * ((step[:, None] * step[None, :]) % LANES) / LANES
    cos, sin = np.cos(angle), np.sin(angle)
    forward = np.block([[cos, -sin], [sin, cos]])
    inverse = np.block([[cos, sin], [-sin, cos]]) / (64.0 * LANES)
    turn = 2.0 * np.pi * (np.arange(BINS, dtype=np.float64)[:, None] * step[None, :]) / (64.0 * LANES)
    twist = np.concatenate([np.cos(turn), np.sin(turn)], axis=1)
    return (
        jnp.asarray(forward, jnp.bfloat16),
        jnp.asarray(inverse, jnp.bfloat16),
        jnp.asarray(twist, jnp.float32),
        jnp.asarray(np.eye(LANES), jnp.bfloat16),
    )


def add(a, b):
    return (a[0] + b[0], a[1] + b[1])


def sub(a, b):
    return (a[0] - b[0], a[1] - b[1])


def turned(a, part):
    part = part % 1.0
    if part == 0.0:
        return a
    if part == 0.25:
        return (-a[1], a[0])
    if part == 0.5:
        return (-a[0], -a[1])
    if part == 0.75:
        return (a[1], -a[0])
    cos, sin = math.cos(2.0 * math.pi * part), math.sin(2.0 * math.pi * part)
    if part in (0.125, 0.375, 0.625, 0.875):
        c, s = math.copysign(1.0, cos), math.copysign(1.0, sin)
        real = a[0] - a[1] if c == s else a[0] + a[1]
        imag = a[0] + a[1] if c == s else a[1] - a[0]
        return ((c * ROOT) * real, (c * ROOT) * imag)
    return (a[0] * cos - a[1] * sin, a[0] * sin + a[1] * cos)


def four(x, sign):
    a, b = add(x[0], x[2]), sub(x[0], x[2])
    c, d = add(x[1], x[3]), sub(x[1], x[3])
    e = turned(d, 0.25 * sign)
    return [add(a, c), add(b, e), sub(a, c), sub(b, e)]


def eight(x, sign):
    even, odd = four(x[0::2], sign), four(x[1::2], sign)
    odd = [turned(odd[k], sign * k / 8.0) for k in range(4)]
    return [add(even[k], odd[k]) for k in range(4)] + [sub(even[k], odd[k]) for k in range(4)]


def real_eight(x):
    a, b = x[0] + x[4], x[0] - x[4]
    c, d = x[2] + x[6], x[2] - x[6]
    e, f = x[1] + x[5], x[1] - x[5]
    g, h = x[3] + x[7], x[3] - x[7]
    p, q = ROOT * (f - h), ROOT * (f + h)
    return [
        (a + c) + (e + g),
        (b + p, -d - q),
        (a - c, g - e),
        (b - p, d - q),
        (a + c) - (e + g),
    ]


def block_forward(x):
    cols = [[] for _ in range(5)]
    for b in range(8):
        x0, x1, x2, x3 = x[b], x[8 + b], x[16 + b], x[24 + b]
        p, q = x0 + x2, x1 + x3
        m, n = ROOT * (x1 - x3), ROOT * q
        cols[0].append(p + q)
        cols[1].append(turned((x0 + m, -x2 - n), -b / 64.0))
        cols[2].append(turned((x0 - x2, x3 - x1), -2 * b / 64.0))
        cols[3].append(turned((x0 - m, x2 - n), -3 * b / 64.0))
        cols[4].append(p - q)
    out = [None] * BINS
    for d, value in enumerate(real_eight(cols[0])):
        out[8 * d] = value
    for c in (1, 2, 3):
        for d, value in enumerate(eight(cols[c], -1)):
            k = c + 8 * d
            if k <= 32:
                out[k] = value
            else:
                out[64 - k] = (value[0], -value[1])
    r = cols[4]
    u = four([turned((r[b], -r[b + 4]), -b / 16.0) for b in range(4)], -1)
    out[4], out[20] = u[0], u[1]
    out[28] = (u[2][0], -u[2][1])
    out[12] = (u[3][0], -u[3][1])
    return out


def real_back(t0, t1, t2, t3, t4, count):
    a, b = t0 + t4, t0 - t4
    r2, i2 = 2.0 * t2[0], 2.0 * t2[1]
    even = [a + r2, b - i2, a - r2, b + i2]
    odd = [
        2.0 * (t1[0] + t3[0]),
        (2.0 * ROOT) * ((t1[0] - t1[1]) - (t3[0] + t3[1])),
        2.0 * (t3[1] - t1[1]),
        (2.0 * ROOT) * ((t3[0] - t3[1]) - (t1[0] + t1[1])),
    ]
    first = [even[k] + odd[k] for k in range(4)]
    if count == 4:
        return first
    return first + [even[k] - odd[k] for k in range(4)]


def block_inverse(v):
    t = [None] * 5
    t[0] = real_back(v[0], v[8], v[16], v[24], v[32], 8)
    for c in (1, 2, 3):
        u = []
        for d in range(8):
            k = c + 8 * d
            u.append(v[k] if k <= 32 else (v[64 - k][0], -v[64 - k][1]))
        u = eight(u, 1)
        t[c] = [turned(u[b], b * c / 64.0) for b in range(8)]
    g = four([v[4], v[20], (v[28][0], -v[28][1]), (v[12][0], -v[12][1])], 1)
    g = [turned(g[b], b / 16.0) for b in range(4)]
    t[4] = [2.0 * g[b][0] for b in range(4)] + [-2.0 * g[b][1] for b in range(4)]
    out = [None] * HALF
    for b in range(8):
        for a, value in enumerate(real_back(t[0][b], t[1][b], t[2][b], t[3][b], t[4][b], 4)):
            out[8 * a + b] = value
    return out


def analyse(read, twist, packed, channels):
    def body(g, carry):
        rows = pl.ds(pl.multiple_of(g * GROUP, GROUP), GROUP)
        bins = block_forward([read(j, rows) for j in range(HALF)])
        for k in range(BINS):
            if k == 0:
                real, imag = bins[0], jnp.zeros_like(bins[0])
            else:
                cos, sin = twist[k : k + 1, :LANES], twist[k : k + 1, LANES:]
                if k == 32:
                    real, imag = bins[k] * cos, -(bins[k] * sin)
                else:
                    real = bins[k][0] * cos + bins[k][1] * sin
                    imag = bins[k][1] * cos - bins[k][0] * sin
            packed[k, rows, :LANES] = real.astype(jnp.bfloat16)
            packed[k, rows, LANES:] = imag.astype(jnp.bfloat16)
        return carry

    lax.fori_loop(0, channels // GROUP, body, 0)


def synthesise(wide, twist, write, channels):
    def body(g, carry):
        rows = pl.ds(pl.multiple_of(g * GROUP, GROUP), GROUP)
        bins = []
        for k in range(BINS):
            real, imag = wide[k, rows, :LANES], wide[k, rows, LANES:]
            cos, sin = twist[k : k + 1, :LANES], twist[k : k + 1, LANES:]
            if k == 0:
                bins.append(real)
            elif k == 32:
                bins.append(real * cos - imag * sin)
            else:
                bins.append((real * cos - imag * sin, real * sin + imag * cos))
        for j, value in enumerate(block_inverse(bins)):
            write(j, rows, value)
        return carry

    lax.fori_loop(0, channels // GROUP, body, 0)


def chunks(body):
    def step(i, carry):
        body(pl.ds(i * CHUNK, CHUNK))
        return carry

    lax.fori_loop(0, BINS // CHUNK, step, 0)


def times(rows, matrix):
    flat = rows.reshape(-1, 2 * LANES)
    out = jnp.dot(flat, matrix, preferred_element_type=jnp.float32)
    return out.reshape(rows.shape)


def times_conj(a, b):
    ar, ai, br, bi = a[..., :LANES], a[..., LANES:], b[..., :LANES], b[..., LANES:]
    return jnp.concatenate([ar * br + ai * bi, ar * bi - ai * br], axis=-1)


def times_plain(a, b):
    ar, ai, br, bi = a[..., :LANES], a[..., LANES:], b[..., :LANES], b[..., LANES:]
    return jnp.concatenate([ar * br - ai * bi, ar * bi + ai * br], axis=-1)


def mixing(
    peers,
    scale,
    query,
    key,
    value,
    grad,
    taps_in,
    forward_in,
    inverse_in,
    twist_in,
    diagonal_in,
    gate,
    mixed_out,
    query_grad,
    back,
    filter_out,
    conv,
    taps,
    forward,
    inverse,
    twist,
    diagonal,
    sent,
    got,
    replied,
    packed,
    wide,
    filter_spec,
    mixed_spec,
    grad_spec,
    term,
    term_got,
    half,
    half_got,
    load_sem,
    send_sem,
    recv_sem,
    term_sem,
    half_sem,
):
    me = lax.axis_index("ctx")
    dp = lax.axis_index("dp")
    line, side = dp // 2, dp % 2
    channels = taps.shape[0]

    barrier = pltpu.get_barrier_semaphore()

    def greet(i, carry):
        pl.semaphore_signal(
            barrier, inc=1, device_id={"ctx": lax.rem(me + i, peers)}, device_id_type=MESH
        )
        return carry

    lax.fori_loop(1, peers, greet, 0)
    for i in range(1, 4):
        pl.semaphore_signal(
            barrier, inc=1, device_id={"dp": lax.rem(line + i, 4) * 2 + side}, device_id_type=MESH
        )
    pl.semaphore_signal(barrier, inc=1, device_id={"dp": line * 2 + 1 - side}, device_id_type=MESH)

    loads = [
        pltpu.make_async_copy(source, target, load_sem.at[n])
        for n, (source, target) in enumerate(
            [
                (key, gate.at[0]),
                (value, gate.at[1]),
                (query, gate.at[2]),
                (grad, gate.at[3]),
                (taps_in, taps),
                (forward_in, forward),
                (inverse_in, inverse),
                (twist_in, twist),
                (diagonal_in, diagonal),
            ]
        )
    ]
    for load in loads:
        load.start()

    def gated(first, second, slot):
        def body(t, carry):
            lanes = pl.ds(pl.multiple_of(t * LANES, LANES), LANES)
            product = gate[first, :, lanes].astype(jnp.float32) * gate[second, :, lanes].astype(jnp.float32)
            flipped = lax.dot_general(
                diagonal[...],
                product.astype(jnp.bfloat16),
                (((1,), (1,)), ((), ())),
                preferred_element_type=jnp.float32,
            ).astype(jnp.bfloat16)
            sent[slot, pl.ds(2 * t, 2)] = flipped.reshape(2, LANES // 2, LANES)
            return carry

        lax.fori_loop(0, peers // 2, body, 0)
        got[slot, me] = sent[slot, me]

    def scatter(source, target, n):
        def body(i, carry):
            peer = lax.rem(me + i, peers)
            pltpu.make_async_remote_copy(
                src_ref=source.at[peer],
                dst_ref=target.at[me],
                send_sem=send_sem.at[n],
                recv_sem=recv_sem.at[n],
                device_id={"ctx": peer},
                device_id_type=MESH,
            ).start()
            return carry

        lax.fori_loop(1, peers, body, 0)

    def whole(source, target, n):
        part = pl.ds(0, peers - 1)
        return pltpu.make_async_remote_copy(
            src_ref=source.at[part],
            dst_ref=target.at[part],
            send_sem=send_sem.at[n],
            recv_sem=recv_sem.at[n],
            device_id={"ctx": lax.rem(me + 1, peers)},
            device_id_type=MESH,
        )

    loads[0].wait()
    loads[1].wait()
    loads[8].wait()
    gated(0, 1, 0)
    pl.semaphore_wait(barrier, peers - 1 + 4)
    scatter(sent.at[0], got.at[0], 0)
    loads[2].wait()
    loads[3].wait()
    gated(2, 3, 1)
    scatter(sent.at[1], got.at[1], 1)
    for load in loads[4:8]:
        load.wait()

    analyse(lambda j, rows: taps[rows, j * LANES : (j + 1) * LANES], twist, packed, channels)

    def filter_step(k):
        filter_spec[k] = times(packed[k], forward[...])

    chunks(filter_step)

    def convolve(slot, spectrum, product, answer):
        whole(sent.at[slot], got.at[slot], slot).wait_recv()
        analyse(lambda j, rows: got[slot, j, rows, :].astype(jnp.float32), twist, packed, channels)

        def step(k):
            spec = times(packed[k], forward[...])
            spectrum[k] = spec
            wide[k] = times(product(filter_spec[k], spec).astype(jnp.bfloat16), inverse[...])

        chunks(step)

        def write(j, rows, values):
            replied[slot, j, rows, :] = values.astype(jnp.bfloat16)

        synthesise(wide, twist, write, channels)
        answer[me] = replied[slot, me]
        scatter(replied.at[slot], answer, slot + 2)

    convolve(0, mixed_spec, times_plain, conv)
    convolve(1, grad_spec, times_conj, back)

    def term_step(k):
        wide[k] = times(times_conj(mixed_spec[k], grad_spec[k]).astype(jnp.bfloat16), inverse[...])

    chunks(term_step)

    def write_term(j, rows, values):
        term[j, rows, :] = values.astype(jnp.bfloat16)

    synthesise(wide, twist, write_term, channels)

    hops = []
    for i in range(1, 4):
        other = lax.rem(line + i, 4)
        hops.append(
            pltpu.make_async_remote_copy(
                src_ref=term.at[pl.ds(other * 8, 8)],
                dst_ref=term_got.at[i - 1],
                send_sem=term_sem.at[i - 1],
                recv_sem=term_sem.at[i + 2],
                device_id={"dp": other * 2 + side},
                device_id_type=MESH,
            )
        )
    for hop in hops:
        hop.start()

    def total(which):
        mine = term[pl.ds(line * 8 + which * 4, 4)].astype(jnp.float32)
        for i in range(3):
            mine += term_got[i, pl.ds(which * 4, 4)].astype(jnp.float32)
        return mine

    for hop in hops:
        hop.wait_recv()
    half[...] = total(1 - side).astype(jnp.bfloat16)
    cross = pltpu.make_async_remote_copy(
        src_ref=half,
        dst_ref=half_got,
        send_sem=half_sem.at[0],
        recv_sem=half_sem.at[1],
        device_id={"dp": line * 2 + 1 - side},
        device_id_type=MESH,
    )
    cross.start()
    kept = total(side)
    for j in range(4):
        filter_out[:, j * LANES : (j + 1) * LANES] = kept[j]

    whole(replied.at[0], conv, 2).wait_recv()

    def conv_tile(t, carry):
        lanes = pl.ds(pl.multiple_of(t * LANES, LANES), LANES)
        columns = turned_over(diagonal[...], conv[pl.ds(2 * t, 2)].reshape(LANES, LANES))
        mixed_out[:, lanes] = (gate[2, :, lanes].astype(jnp.float32) * columns).astype(jnp.bfloat16)
        query_grad[:, lanes] = (gate[3, :, lanes].astype(jnp.float32) * columns).astype(jnp.bfloat16)
        return carry

    lax.fori_loop(0, peers // 2, conv_tile, 0)
    cross.wait_recv()
    for j in range(4):
        lanes = slice(j * LANES, (j + 1) * LANES)
        filter_out[:, lanes] = (filter_out[:, lanes] + half_got[j].astype(jnp.float32)) * scale
    for slot in range(2):
        whole(sent.at[slot], got.at[slot], slot).wait_send()
    whole(replied.at[0], conv, 2).wait_send()
    for hop in hops:
        hop.wait_send()
    cross.wait_send()
    whole(replied.at[1], back, 3).wait()


def turned_over(identity, rows):
    return lax.dot_general(identity, rows, (((1,), (1,)), ((), ())), preferred_element_type=jnp.float32)


def finish(steps, gate, mixed, query, back, total, mixed_out, query_grad, key_grad, value_grad, filter_grad, made, sem):
    block, width = mixed.shape
    rows = block // PIECES
    copies = []

    def send(source, target):
        copies.append(pltpu.make_async_copy(source, target, sem.at[len(copies)]))
        copies[-1].start()

    for held, out in ((mixed, mixed_out), (query, query_grad)):
        for n in range(PIECES):
            part = pl.ds(n * rows, rows)
            send(held.at[part], out.at[0, part])
    send(total, filter_grad)
    identity = lax.broadcasted_iota(jnp.int32, (block, block), 0) == lax.broadcasted_iota(
        jnp.int32, (block, block), 1
    )
    identity = identity.astype(jnp.float32).astype(jnp.bfloat16)
    owners = back.shape[0] // steps
    for n in range(steps):
        lanes = pl.ds(n * (width // steps), width // steps)
        columns = turned_over(identity, back[n * owners : (n + 1) * owners].reshape(-1, block))
        for slot, factor, out in ((0, 1, key_grad), (1, 0, value_grad)):
            made[slot, :, lanes] = (columns * gate[factor, :, lanes].astype(jnp.float32)).astype(jnp.bfloat16)
            send(made.at[slot, :, lanes], out.at[0, :, lanes])
    for copy in copies:
        copy.wait()


def shards(query_gate, key_gate, value_in, out_grad, filter_taps):
    _, block, width = query_gate.shape
    channels, seq_len = filter_taps.shape
    peers = lax.axis_size("ctx")
    parts = lax.axis_size("dp")
    forward, inverse, twist, diagonal = tables()
    in_hbm = pl.BlockSpec(memory_space=pltpu.HBM)
    in_vmem = pl.BlockSpec(memory_space=pltpu.VMEM)
    planes = (peers, channels, LANES)
    spectrum = pltpu.VMEM((BINS, channels, 2 * LANES), jnp.float32)
    share = seq_len // parts
    tokens = jax.ShapeDtypeStruct(query_gate.shape, jnp.bfloat16)
    filter_share = jax.ShapeDtypeStruct((channels, share), jnp.float32)
    held = pl.pallas_call(
        functools.partial(mixing, peers, (seq_len * parts) ** (-0.5)),
        out_shape=(
            pltpu.VMEM((4, block, width), jnp.bfloat16),
            pltpu.VMEM((block, width), jnp.bfloat16),
            pltpu.VMEM((block, width), jnp.bfloat16),
            pltpu.VMEM(planes, jnp.bfloat16),
            pltpu.VMEM(filter_share.shape, filter_share.dtype),
        ),
        in_specs=[in_hbm] * 9,
        out_specs=(in_vmem,) * 5,
        scratch_shapes=[
            pltpu.VMEM(planes, jnp.bfloat16),
            pltpu.VMEM((channels, seq_len), jnp.float32),
            pltpu.VMEM((2 * LANES, 2 * LANES), jnp.bfloat16),
            pltpu.VMEM((2 * LANES, 2 * LANES), jnp.bfloat16),
            pltpu.VMEM((BINS, 2 * LANES), jnp.float32),
            pltpu.VMEM((LANES, LANES), jnp.bfloat16),
            pltpu.VMEM((2,) + planes, jnp.bfloat16),
            pltpu.VMEM((2,) + planes, jnp.bfloat16),
            pltpu.VMEM((2,) + planes, jnp.bfloat16),
            pltpu.VMEM((BINS, channels, 2 * LANES), jnp.bfloat16),
            spectrum,
            spectrum,
            spectrum,
            spectrum,
            pltpu.VMEM(planes, jnp.bfloat16),
            pltpu.VMEM((3, 8, channels, LANES), jnp.bfloat16),
            pltpu.VMEM((4, channels, LANES), jnp.bfloat16),
            pltpu.VMEM((4, channels, LANES), jnp.bfloat16),
            pltpu.SemaphoreType.DMA((9,)),
            pltpu.SemaphoreType.DMA((4,)),
            pltpu.SemaphoreType.DMA((4,)),
            pltpu.SemaphoreType.DMA((6,)),
            pltpu.SemaphoreType.DMA((2,)),
        ],
        compiler_params=pltpu.CompilerParams(
            collective_id=0, has_side_effects=True, vmem_limit_bytes=32 << 20
        ),
        name="mixing",
    )(
        *(
            pltpu.with_memory_space_constraint(a, pltpu.HBM)
            for a in (
                query_gate[0],
                key_gate[0],
                value_in[0],
                out_grad[0],
                filter_taps,
                forward,
                inverse,
                twist,
                diagonal,
            )
        )
    )

    steps = 4
    return pl.pallas_call(
        functools.partial(finish, steps),
        out_shape=tuple(pltpu.HBM(a.shape, a.dtype) for a in (tokens,) * 4 + (filter_share,)),
        in_specs=[in_vmem] * 5,
        out_specs=(in_hbm,) * 5,
        scratch_shapes=[
            pltpu.VMEM((2, block, width), jnp.bfloat16),
            pltpu.SemaphoreType.DMA((2 * PIECES + 1 + 2 * steps,)),
        ],
        compiler_params=pltpu.CompilerParams(vmem_limit_bytes=16 << 20),
        name="finish",
    )(*(pltpu.with_memory_space_constraint(a, pltpu.VMEM) for a in held))


def solution(mesh):
    placed = (
        P("dp", "ctx", None),
        P("dp", "ctx", None),
        P("dp", "ctx", None),
        P("dp", "ctx", None),
        P("ctx", None),
    )
    return jax.shard_map(
        shards,
        mesh=mesh,
        in_specs=placed,
        out_specs=(
            P("dp", "ctx", None),
            P("dp", "ctx", None),
            P("dp", "ctx", None),
            P("dp", "ctx", None),
            P("ctx", "dp"),
        ),
        check_vma=False,
    )
```

```python
import functools
import math

import jax
import jax.numpy as jnp
import numpy as np
from jax import lax
from jax.experimental import pallas as pl
from jax.experimental.pallas import tpu as pltpu
from jax.sharding import PartitionSpec as P

MESH = pl.DeviceIdType.MESH
LANES = 128
HALF = 32
BINS = 33
GROUP = 16
CHUNK = 11
PIECES = 2
ROOT = math.sqrt(0.5)


def in_two(matrix):
    high = matrix.astype(jnp.bfloat16)
    return jnp.asarray(np.stack([high, (matrix - high.astype(np.float64)).astype(jnp.bfloat16)]))


def tables():
    step = np.arange(LANES, dtype=np.float64)
    angle = 2.0 * np.pi * ((step[:, None] * step[None, :]) % LANES) / LANES
    cos, sin = np.cos(angle), np.sin(angle)
    forward = np.block([[cos, -sin], [sin, cos]])
    inverse = np.block([[cos, sin], [-sin, cos]]) / (64.0 * LANES)
    turn = 2.0 * np.pi * (np.arange(BINS, dtype=np.float64)[:, None] * step[None, :]) / (64.0 * LANES)
    twist = np.concatenate([np.cos(turn), np.sin(turn)], axis=1)
    return (
        in_two(forward),
        in_two(inverse),
        jnp.asarray(twist, jnp.float32),
        jnp.asarray(np.eye(LANES), jnp.bfloat16),
    )


def add(a, b):
    return (a[0] + b[0], a[1] + b[1])


def sub(a, b):
    return (a[0] - b[0], a[1] - b[1])


def turned(a, part):
    part = part % 1.0
    if part == 0.0:
        return a
    if part == 0.25:
        return (-a[1], a[0])
    if part == 0.5:
        return (-a[0], -a[1])
    if part == 0.75:
        return (a[1], -a[0])
    cos, sin = math.cos(2.0 * math.pi * part), math.sin(2.0 * math.pi * part)
    if part in (0.125, 0.375, 0.625, 0.875):
        c, s = math.copysign(1.0, cos), math.copysign(1.0, sin)
        real = a[0] - a[1] if c == s else a[0] + a[1]
        imag = a[0] + a[1] if c == s else a[1] - a[0]
        return ((c * ROOT) * real, (c * ROOT) * imag)
    return (a[0] * cos - a[1] * sin, a[0] * sin + a[1] * cos)


def four(x, sign):
    a, b = add(x[0], x[2]), sub(x[0], x[2])
    c, d = add(x[1], x[3]), sub(x[1], x[3])
    e = turned(d, 0.25 * sign)
    return [add(a, c), add(b, e), sub(a, c), sub(b, e)]


def eight(x, sign):
    even, odd = four(x[0::2], sign), four(x[1::2], sign)
    odd = [turned(odd[k], sign * k / 8.0) for k in range(4)]
    return [add(even[k], odd[k]) for k in range(4)] + [sub(even[k], odd[k]) for k in range(4)]


def real_eight(x):
    a, b = x[0] + x[4], x[0] - x[4]
    c, d = x[2] + x[6], x[2] - x[6]
    e, f = x[1] + x[5], x[1] - x[5]
    g, h = x[3] + x[7], x[3] - x[7]
    p, q = ROOT * (f - h), ROOT * (f + h)
    return [
        (a + c) + (e + g),
        (b + p, -d - q),
        (a - c, g - e),
        (b - p, d - q),
        (a + c) - (e + g),
    ]


def block_forward(x):
    cols = [[] for _ in range(5)]
    for b in range(8):
        x0, x1, x2, x3 = x[b], x[8 + b], x[16 + b], x[24 + b]
        p, q = x0 + x2, x1 + x3
        m, n = ROOT * (x1 - x3), ROOT * q
        cols[0].append(p + q)
        cols[1].append(turned((x0 + m, -x2 - n), -b / 64.0))
        cols[2].append(turned((x0 - x2, x3 - x1), -2 * b / 64.0))
        cols[3].append(turned((x0 - m, x2 - n), -3 * b / 64.0))
        cols[4].append(p - q)
    out = [None] * BINS
    for d, value in enumerate(real_eight(cols[0])):
        out[8 * d] = value
    for c in (1, 2, 3):
        for d, value in enumerate(eight(cols[c], -1)):
            k = c + 8 * d
            if k <= 32:
                out[k] = value
            else:
                out[64 - k] = (value[0], -value[1])
    r = cols[4]
    u = four([turned((r[b], -r[b + 4]), -b / 16.0) for b in range(4)], -1)
    out[4], out[20] = u[0], u[1]
    out[28] = (u[2][0], -u[2][1])
    out[12] = (u[3][0], -u[3][1])
    return out


def real_back(t0, t1, t2, t3, t4, count):
    a, b = t0 + t4, t0 - t4
    r2, i2 = 2.0 * t2[0], 2.0 * t2[1]
    even = [a + r2, b - i2, a - r2, b + i2]
    odd = [
        2.0 * (t1[0] + t3[0]),
        (2.0 * ROOT) * ((t1[0] - t1[1]) - (t3[0] + t3[1])),
        2.0 * (t3[1] - t1[1]),
        (2.0 * ROOT) * ((t3[0] - t3[1]) - (t1[0] + t1[1])),
    ]
    first = [even[k] + odd[k] for k in range(4)]
    if count == 4:
        return first
    return first + [even[k] - odd[k] for k in range(4)]


def block_inverse(v):
    t = [None] * 5
    t[0] = real_back(v[0], v[8], v[16], v[24], v[32], 8)
    for c in (1, 2, 3):
        u = []
        for d in range(8):
            k = c + 8 * d
            u.append(v[k] if k <= 32 else (v[64 - k][0], -v[64 - k][1]))
        u = eight(u, 1)
        t[c] = [turned(u[b], b * c / 64.0) for b in range(8)]
    g = four([v[4], v[20], (v[28][0], -v[28][1]), (v[12][0], -v[12][1])], 1)
    g = [turned(g[b], b / 16.0) for b in range(4)]
    t[4] = [2.0 * g[b][0] for b in range(4)] + [-2.0 * g[b][1] for b in range(4)]
    out = [None] * HALF
    for b in range(8):
        for a, value in enumerate(real_back(t[0][b], t[1][b], t[2][b], t[3][b], t[4][b], 4)):
            out[8 * a + b] = value
    return out


def analyse(read, twist, packed, channels):
    def body(g, carry):
        rows = pl.ds(pl.multiple_of(g * GROUP, GROUP), GROUP)
        bins = block_forward([read(j, rows) for j in range(HALF)])
        for k in range(BINS):
            if k == 0:
                real, imag = bins[0], jnp.zeros_like(bins[0])
            else:
                cos, sin = twist[k : k + 1, :LANES], twist[k : k + 1, LANES:]
                if k == 32:
                    real, imag = bins[k] * cos, -(bins[k] * sin)
                else:
                    real = bins[k][0] * cos + bins[k][1] * sin
                    imag = bins[k][1] * cos - bins[k][0] * sin
            packed[k, rows, :LANES] = real
            packed[k, rows, LANES:] = imag
        return carry

    lax.fori_loop(0, channels // GROUP, body, 0)


def synthesise(wide, twist, write, channels):
    def body(g, carry):
        rows = pl.ds(pl.multiple_of(g * GROUP, GROUP), GROUP)
        bins = []
        for k in range(BINS):
            real, imag = wide[k, rows, :LANES], wide[k, rows, LANES:]
            cos, sin = twist[k : k + 1, :LANES], twist[k : k + 1, LANES:]
            if k == 0:
                bins.append(real)
            elif k == 32:
                bins.append(real * cos - imag * sin)
            else:
                bins.append((real * cos - imag * sin, real * sin + imag * cos))
        for j, value in enumerate(block_inverse(bins)):
            write(j, rows, value)
        return carry

    lax.fori_loop(0, channels // GROUP, body, 0)


def grouped(count, size, body):
    def step(i, carry):
        for n in range(size):
            body(i * size + n, 0)
        return carry

    lax.fori_loop(0, count // size, step, 0)


def chunks(body):
    def step(i, carry):
        body(pl.ds(i * CHUNK, CHUNK))
        return carry

    lax.fori_loop(0, BINS // CHUNK, step, 0)


def times(rows, matrix):
    flat = rows.reshape(-1, 2 * LANES)
    high = flat.astype(jnp.bfloat16)
    low = (flat - high.astype(jnp.float32)).astype(jnp.bfloat16)
    out = jnp.dot(high, matrix[0], preferred_element_type=jnp.float32)
    out += jnp.dot(high, matrix[1], preferred_element_type=jnp.float32)
    out += jnp.dot(low, matrix[0], preferred_element_type=jnp.float32)
    return out.reshape(rows.shape)


def times_conj(a, b):
    ar, ai, br, bi = a[..., :LANES], a[..., LANES:], b[..., :LANES], b[..., LANES:]
    return jnp.concatenate([ar * br + ai * bi, ar * bi - ai * br], axis=-1)


def times_plain(a, b):
    ar, ai, br, bi = a[..., :LANES], a[..., LANES:], b[..., :LANES], b[..., LANES:]
    return jnp.concatenate([ar * br - ai * bi, ar * bi + ai * br], axis=-1)


def mixing(
    peers,
    scale,
    query,
    key,
    value,
    grad,
    taps_in,
    forward_in,
    inverse_in,
    twist_in,
    diagonal_in,
    gate,
    mixed_out,
    query_grad,
    back,
    filter_out,
    conv,
    taps,
    forward,
    inverse,
    twist,
    diagonal,
    sent,
    got,
    replied,
    packed,
    wide,
    filter_spec,
    mixed_spec,
    grad_spec,
    term,
    term_got,
    half,
    half_got,
    load_sem,
    send_sem,
    recv_sem,
    term_sem,
    half_sem,
):
    me = lax.axis_index("ctx")
    dp = lax.axis_index("dp")
    line, side = dp // 2, dp % 2
    channels = taps.shape[0]

    barrier = pltpu.get_barrier_semaphore()

    loads = [
        pltpu.make_async_copy(source, target, load_sem.at[n])
        for n, (source, target) in enumerate(
            [
                (key, gate.at[0]),
                (value, gate.at[1]),
                (query, gate.at[2]),
                (grad, gate.at[3]),
                (taps_in, taps),
                (forward_in, forward),
                (inverse_in, inverse),
                (twist_in, twist),
                (diagonal_in, diagonal),
            ]
        )
    ]
    for load in loads[:2] + loads[8:]:
        load.start()

    for i in range(1, peers):
        pl.semaphore_signal(barrier, inc=1, device_id={"ctx": lax.rem(me + i, peers)}, device_id_type=MESH)
    for i in range(1, 4):
        pl.semaphore_signal(
            barrier, inc=1, device_id={"dp": lax.rem(line + i, 4) * 2 + side}, device_id_type=MESH
        )
    pl.semaphore_signal(barrier, inc=1, device_id={"dp": line * 2 + 1 - side}, device_id_type=MESH)

    def gated(first, second, slot):
        def body(t, carry):
            lanes = pl.ds(pl.multiple_of(t * LANES, LANES), LANES)
            product = gate[first, :, lanes].astype(jnp.float32) * gate[second, :, lanes].astype(jnp.float32)
            flipped = lax.dot_general(
                diagonal[...],
                product.astype(jnp.bfloat16),
                (((1,), (1,)), ((), ())),
                preferred_element_type=jnp.float32,
            ).astype(jnp.bfloat16)
            sent[slot, pl.ds(2 * t, 2)] = flipped.reshape(2, LANES // 2, LANES)
            return carry

        grouped(peers // 2, 4, body)
        got[slot, me] = sent[slot, me]

    def scatter(source, target, n):
        def body(i, carry):
            peer = lax.rem(me + i, peers)
            pltpu.make_async_remote_copy(
                src_ref=source.at[peer],
                dst_ref=target.at[me],
                send_sem=send_sem.at[n],
                recv_sem=recv_sem.at[n],
                device_id={"ctx": peer},
                device_id_type=MESH,
            ).start()
            return carry

        lax.fori_loop(1, peers, body, 0)

    def whole(source, target, n):
        part = pl.ds(0, peers - 1)
        return pltpu.make_async_remote_copy(
            src_ref=source.at[part],
            dst_ref=target.at[part],
            send_sem=send_sem.at[n],
            recv_sem=recv_sem.at[n],
            device_id={"ctx": lax.rem(me + 1, peers)},
            device_id_type=MESH,
        )

    loads[0].wait()
    loads[1].wait()
    loads[8].wait()
    for load in loads[2:8]:
        load.start()
    gated(0, 1, 0)
    pl.semaphore_wait(barrier, peers - 1 + 4)
    scatter(sent.at[0], got.at[0], 0)
    loads[2].wait()
    loads[3].wait()
    gated(2, 3, 1)
    scatter(sent.at[1], got.at[1], 1)
    for load in loads[4:8]:
        load.wait()

    analyse(lambda j, rows: taps[rows, j * LANES : (j + 1) * LANES], twist, packed, channels)

    def filter_step(k):
        filter_spec[k] = times(packed[k], forward)

    chunks(filter_step)

    def convolve(slot, spectrum, product, answer):
        whole(sent.at[slot], got.at[slot], slot).wait_recv()
        analyse(lambda j, rows: got[slot, j, rows, :].astype(jnp.float32), twist, packed, channels)

        def step(k):
            spec = times(packed[k], forward)
            spectrum[k] = spec
            wide[k] = times(product(filter_spec[k], spec), inverse)

        chunks(step)

        def write(j, rows, values):
            replied[slot, j, rows, :] = values.astype(jnp.bfloat16)

        synthesise(wide, twist, write, channels)
        answer[me] = replied[slot, me]
        scatter(replied.at[slot], answer, slot + 2)

    convolve(0, mixed_spec, times_plain, conv)
    convolve(1, grad_spec, times_conj, back)

    def term_step(k):
        wide[k] = times(times_conj(mixed_spec[k], grad_spec[k]), inverse)

    chunks(term_step)

    def write_term(j, rows, values):
        term[j, rows, :] = values.astype(jnp.bfloat16)

    synthesise(wide, twist, write_term, channels)

    hops = []
    for i in range(1, 4):
        other = lax.rem(line + i, 4)
        hops.append(
            pltpu.make_async_remote_copy(
                src_ref=term.at[pl.ds(other * 8, 8)],
                dst_ref=term_got.at[i - 1],
                send_sem=term_sem.at[i - 1],
                recv_sem=term_sem.at[i + 2],
                device_id={"dp": other * 2 + side},
                device_id_type=MESH,
            )
        )
    for hop in hops:
        hop.start()

    def total(which):
        mine = term[pl.ds(line * 8 + which * 4, 4)].astype(jnp.float32)
        for i in range(3):
            mine += term_got[i, pl.ds(which * 4, 4)].astype(jnp.float32)
        return mine

    for hop in hops:
        hop.wait_recv()
    half[...] = total(1 - side).astype(jnp.bfloat16)
    cross = pltpu.make_async_remote_copy(
        src_ref=half,
        dst_ref=half_got,
        send_sem=half_sem.at[0],
        recv_sem=half_sem.at[1],
        device_id={"dp": line * 2 + 1 - side},
        device_id_type=MESH,
    )
    cross.start()
    kept = total(side)
    for j in range(4):
        filter_out[:, j * LANES : (j + 1) * LANES] = kept[j]

    whole(replied.at[0], conv, 2).wait_recv()

    def conv_tile(t, carry):
        lanes = pl.ds(pl.multiple_of(t * LANES, LANES), LANES)
        columns = turned_over(diagonal[...], conv[pl.ds(2 * t, 2)].reshape(LANES, LANES))
        mixed_out[:, lanes] = (gate[2, :, lanes].astype(jnp.float32) * columns).astype(jnp.bfloat16)
        query_grad[:, lanes] = (gate[3, :, lanes].astype(jnp.float32) * columns).astype(jnp.bfloat16)
        return carry

    lax.fori_loop(0, peers // 2, conv_tile, 0)
    cross.wait_recv()
    for j in range(4):
        lanes = slice(j * LANES, (j + 1) * LANES)
        filter_out[:, lanes] = (filter_out[:, lanes] + half_got[j].astype(jnp.float32)) * scale
    for slot in range(2):
        whole(sent.at[slot], got.at[slot], slot).wait_send()
    whole(replied.at[0], conv, 2).wait_send()
    for hop in hops:
        hop.wait_send()
    cross.wait_send()
    whole(replied.at[1], back, 3).wait()


def turned_over(identity, rows):
    return lax.dot_general(identity, rows, (((1,), (1,)), ((), ())), preferred_element_type=jnp.float32)


def finish(steps, gate, mixed, query, back, total, mixed_out, query_grad, key_grad, value_grad, filter_grad, made, sem):
    block, width = mixed.shape
    rows = block // PIECES
    copies = []

    def send(source, target):
        copies.append(pltpu.make_async_copy(source, target, sem.at[len(copies)]))
        copies[-1].start()

    for held, out in ((mixed, mixed_out), (query, query_grad)):
        for n in range(PIECES):
            part = pl.ds(n * rows, rows)
            send(held.at[part], out.at[0, part])
    send(total, filter_grad)
    identity = lax.broadcasted_iota(jnp.int32, (block, block), 0) == lax.broadcasted_iota(
        jnp.int32, (block, block), 1
    )
    identity = identity.astype(jnp.float32).astype(jnp.bfloat16)
    owners = back.shape[0] // steps
    for n in range(steps):
        lanes = pl.ds(n * (width // steps), width // steps)
        columns = turned_over(identity, back[n * owners : (n + 1) * owners].reshape(-1, block))
        for slot, factor, out in ((0, 1, key_grad), (1, 0, value_grad)):
            made[slot, :, lanes] = (columns * gate[factor, :, lanes].astype(jnp.float32)).astype(jnp.bfloat16)
            send(made.at[slot, :, lanes], out.at[0, :, lanes])
    for copy in copies:
        copy.wait()


def shards(query_gate, key_gate, value_in, out_grad, filter_taps):
    _, block, width = query_gate.shape
    channels, seq_len = filter_taps.shape
    peers = lax.axis_size("ctx")
    parts = lax.axis_size("dp")
    forward, inverse, twist, diagonal = tables()
    in_hbm = pl.BlockSpec(memory_space=pltpu.HBM)
    in_vmem = pl.BlockSpec(memory_space=pltpu.VMEM)
    planes = (peers, channels, LANES)
    spectrum = pltpu.VMEM((BINS, channels, 2 * LANES), jnp.float32)
    share = seq_len // parts
    tokens = jax.ShapeDtypeStruct(query_gate.shape, jnp.bfloat16)
    filter_share = jax.ShapeDtypeStruct((channels, share), jnp.float32)
    held = pl.pallas_call(
        functools.partial(mixing, peers, (seq_len * parts) ** (-0.5)),
        out_shape=(
            pltpu.VMEM((4, block, width), jnp.bfloat16),
            pltpu.VMEM((block, width), jnp.bfloat16),
            pltpu.VMEM((block, width), jnp.bfloat16),
            pltpu.VMEM(planes, jnp.bfloat16),
            pltpu.VMEM(filter_share.shape, filter_share.dtype),
        ),
        in_specs=[in_hbm] * 9,
        out_specs=(in_vmem,) * 5,
        scratch_shapes=[
            pltpu.VMEM(planes, jnp.bfloat16),
            pltpu.VMEM((channels, seq_len), jnp.float32),
            pltpu.VMEM((2, 2 * LANES, 2 * LANES), jnp.bfloat16),
            pltpu.VMEM((2, 2 * LANES, 2 * LANES), jnp.bfloat16),
            pltpu.VMEM((BINS, 2 * LANES), jnp.float32),
            pltpu.VMEM((LANES, LANES), jnp.bfloat16),
            pltpu.VMEM((2,) + planes, jnp.bfloat16),
            pltpu.VMEM((2,) + planes, jnp.bfloat16),
            pltpu.VMEM((2,) + planes, jnp.bfloat16),
            spectrum,
            spectrum,
            spectrum,
            spectrum,
            spectrum,
            pltpu.VMEM(planes, jnp.bfloat16),
            pltpu.VMEM((3, 8, channels, LANES), jnp.bfloat16),
            pltpu.VMEM((4, channels, LANES), jnp.bfloat16),
            pltpu.VMEM((4, channels, LANES), jnp.bfloat16),
            pltpu.SemaphoreType.DMA((9,)),
            pltpu.SemaphoreType.DMA((4,)),
            pltpu.SemaphoreType.DMA((4,)),
            pltpu.SemaphoreType.DMA((6,)),
            pltpu.SemaphoreType.DMA((2,)),
        ],
        compiler_params=pltpu.CompilerParams(
            collective_id=0, has_side_effects=True, vmem_limit_bytes=32 << 20
        ),
        name="mixing",
    )(
        *(
            pltpu.with_memory_space_constraint(a, pltpu.HBM)
            for a in (
                query_gate[0],
                key_gate[0],
                value_in[0],
                out_grad[0],
                filter_taps,
                forward,
                inverse,
                twist,
                diagonal,
            )
        )
    )

    steps = 4
    return pl.pallas_call(
        functools.partial(finish, steps),
        out_shape=tuple(pltpu.HBM(a.shape, a.dtype) for a in (tokens,) * 4 + (filter_share,)),
        in_specs=[in_vmem] * 5,
        out_specs=(in_hbm,) * 5,
        scratch_shapes=[
            pltpu.VMEM((2, block, width), jnp.bfloat16),
            pltpu.SemaphoreType.DMA((2 * PIECES + 1 + 2 * steps,)),
        ],
        compiler_params=pltpu.CompilerParams(vmem_limit_bytes=16 << 20),
        name="finish",
    )(*(pltpu.with_memory_space_constraint(a, pltpu.VMEM) for a in held))


def solution(mesh):
    placed = (
        P("dp", "ctx", None),
        P("dp", "ctx", None),
        P("dp", "ctx", None),
        P("dp", "ctx", None),
        P("ctx", None),
    )
    return jax.shard_map(
        shards,
        mesh=mesh,
        in_specs=placed,
        out_specs=(
            P("dp", "ctx", None),
            P("dp", "ctx", None),
            P("dp", "ctx", None),
            P("dp", "ctx", None),
            P("ctx", "dp"),
        ),
        check_vma=False,
    )
```

```python
import functools
import math

import jax
import jax.numpy as jnp
import numpy as np
from jax import lax
from jax.experimental import pallas as pl
from jax.experimental.pallas import tpu as pltpu
from jax.sharding import PartitionSpec as P

MESH = pl.DeviceIdType.MESH
LANES = 128
HALF = 32
BINS = 33
GROUP = 16
CHUNK = 11
PIECES = 1
ROOT = math.sqrt(0.5)


def in_two(matrix):
    high = matrix.astype(jnp.bfloat16)
    return jnp.asarray(np.stack([high, (matrix - high.astype(np.float64)).astype(jnp.bfloat16)]))


def tables():
    step = np.arange(LANES, dtype=np.float64)
    angle = 2.0 * np.pi * ((step[:, None] * step[None, :]) % LANES) / LANES
    cos, sin = np.cos(angle), np.sin(angle)
    forward = np.block([[cos, -sin], [sin, cos]])
    inverse = np.block([[cos, sin], [-sin, cos]]) / (64.0 * LANES)
    turn = 2.0 * np.pi * (np.arange(BINS, dtype=np.float64)[:, None] * step[None, :]) / (64.0 * LANES)
    twist = np.concatenate([np.cos(turn), np.sin(turn)], axis=1)
    return (
        in_two(forward),
        in_two(inverse),
        jnp.asarray(twist, jnp.float32),
        jnp.asarray(np.eye(LANES), jnp.bfloat16),
    )


def add(a, b):
    return (a[0] + b[0], a[1] + b[1])


def sub(a, b):
    return (a[0] - b[0], a[1] - b[1])


def turned(a, part):
    part = part % 1.0
    if part == 0.0:
        return a
    if part == 0.25:
        return (-a[1], a[0])
    if part == 0.5:
        return (-a[0], -a[1])
    if part == 0.75:
        return (a[1], -a[0])
    cos, sin = math.cos(2.0 * math.pi * part), math.sin(2.0 * math.pi * part)
    if part in (0.125, 0.375, 0.625, 0.875):
        c, s = math.copysign(1.0, cos), math.copysign(1.0, sin)
        real = a[0] - a[1] if c == s else a[0] + a[1]
        imag = a[0] + a[1] if c == s else a[1] - a[0]
        return ((c * ROOT) * real, (c * ROOT) * imag)
    return (a[0] * cos - a[1] * sin, a[0] * sin + a[1] * cos)


def four(x, sign):
    a, b = add(x[0], x[2]), sub(x[0], x[2])
    c, d = add(x[1], x[3]), sub(x[1], x[3])
    e = turned(d, 0.25 * sign)
    return [add(a, c), add(b, e), sub(a, c), sub(b, e)]


def eight(x, sign):
    even, odd = four(x[0::2], sign), four(x[1::2], sign)
    odd = [turned(odd[k], sign * k / 8.0) for k in range(4)]
    return [add(even[k], odd[k]) for k in range(4)] + [sub(even[k], odd[k]) for k in range(4)]


def real_eight(x):
    a, b = x[0] + x[4], x[0] - x[4]
    c, d = x[2] + x[6], x[2] - x[6]
    e, f = x[1] + x[5], x[1] - x[5]
    g, h = x[3] + x[7], x[3] - x[7]
    p, q = ROOT * (f - h), ROOT * (f + h)
    return [
        (a + c) + (e + g),
        (b + p, -d - q),
        (a - c, g - e),
        (b - p, d - q),
        (a + c) - (e + g),
    ]


def block_forward(x):
    cols = [[] for _ in range(5)]
    for b in range(8):
        x0, x1, x2, x3 = x[b], x[8 + b], x[16 + b], x[24 + b]
        p, q = x0 + x2, x1 + x3
        m, n = ROOT * (x1 - x3), ROOT * q
        cols[0].append(p + q)
        cols[1].append(turned((x0 + m, -x2 - n), -b / 64.0))
        cols[2].append(turned((x0 - x2, x3 - x1), -2 * b / 64.0))
        cols[3].append(turned((x0 - m, x2 - n), -3 * b / 64.0))
        cols[4].append(p - q)
    out = [None] * BINS
    for d, value in enumerate(real_eight(cols[0])):
        out[8 * d] = value
    for c in (1, 2, 3):
        for d, value in enumerate(eight(cols[c], -1)):
            k = c + 8 * d
            if k <= 32:
                out[k] = value
            else:
                out[64 - k] = (value[0], -value[1])
    r = cols[4]
    u = four([turned((r[b], -r[b + 4]), -b / 16.0) for b in range(4)], -1)
    out[4], out[20] = u[0], u[1]
    out[28] = (u[2][0], -u[2][1])
    out[12] = (u[3][0], -u[3][1])
    return out


def real_back(t0, t1, t2, t3, t4, count):
    a, b = t0 + t4, t0 - t4
    r2, i2 = 2.0 * t2[0], 2.0 * t2[1]
    even = [a + r2, b - i2, a - r2, b + i2]
    odd = [
        2.0 * (t1[0] + t3[0]),
        (2.0 * ROOT) * ((t1[0] - t1[1]) - (t3[0] + t3[1])),
        2.0 * (t3[1] - t1[1]),
        (2.0 * ROOT) * ((t3[0] - t3[1]) - (t1[0] + t1[1])),
    ]
    first = [even[k] + odd[k] for k in range(4)]
    if count == 4:
        return first
    return first + [even[k] - odd[k] for k in range(4)]


def block_inverse(v):
    t = [None] * 5
    t[0] = real_back(v[0], v[8], v[16], v[24], v[32], 8)
    for c in (1, 2, 3):
        u = []
        for d in range(8):
            k = c + 8 * d
            u.append(v[k] if k <= 32 else (v[64 - k][0], -v[64 - k][1]))
        u = eight(u, 1)
        t[c] = [turned(u[b], b * c / 64.0) for b in range(8)]
    g = four([v[4], v[20], (v[28][0], -v[28][1]), (v[12][0], -v[12][1])], 1)
    g = [turned(g[b], b / 16.0) for b in range(4)]
    t[4] = [2.0 * g[b][0] for b in range(4)] + [-2.0 * g[b][1] for b in range(4)]
    out = [None] * HALF
    for b in range(8):
        for a, value in enumerate(real_back(t[0][b], t[1][b], t[2][b], t[3][b], t[4][b], 4)):
            out[8 * a + b] = value
    return out


def analyse(read, twist, packed, channels):
    def body(g, carry):
        rows = pl.ds(pl.multiple_of(g * GROUP, GROUP), GROUP)
        bins = block_forward([read(j, rows) for j in range(HALF)])
        for k in range(BINS):
            if k == 0:
                real, imag = bins[0], jnp.zeros_like(bins[0])
            else:
                cos, sin = twist[k : k + 1, :LANES], twist[k : k + 1, LANES:]
                if k == 32:
                    real, imag = bins[k] * cos, -(bins[k] * sin)
                else:
                    real = bins[k][0] * cos + bins[k][1] * sin
                    imag = bins[k][1] * cos - bins[k][0] * sin
            packed[k, rows, :LANES] = real
            packed[k, rows, LANES:] = imag
        return carry

    lax.fori_loop(0, channels // GROUP, body, 0)


def synthesise(wide, twist, write, channels):
    def body(g, carry):
        rows = pl.ds(pl.multiple_of(g * GROUP, GROUP), GROUP)
        bins = []
        for k in range(BINS):
            real, imag = wide[k, rows, :LANES], wide[k, rows, LANES:]
            cos, sin = twist[k : k + 1, :LANES], twist[k : k + 1, LANES:]
            if k == 0:
                bins.append(real)
            elif k == 32:
                bins.append(real * cos - imag * sin)
            else:
                bins.append((real * cos - imag * sin, real * sin + imag * cos))
        for j, value in enumerate(block_inverse(bins)):
            write(j, rows, value)
        return carry

    lax.fori_loop(0, channels // GROUP, body, 0)


def grouped(count, size, body):
    def step(i, carry):
        for n in range(size):
            body(i * size + n, 0)
        return carry

    lax.fori_loop(0, count // size, step, 0)


def chunks(body):
    def step(i, carry):
        body(pl.ds(i * CHUNK, CHUNK))
        return carry

    lax.fori_loop(0, BINS // CHUNK, step, 0)


def times(rows, matrix):
    flat = rows.reshape(-1, 2 * LANES)
    high = flat.astype(jnp.bfloat16)
    low = (flat - high.astype(jnp.float32)).astype(jnp.bfloat16)
    out = jnp.dot(high, matrix[0], preferred_element_type=jnp.float32)
    out += jnp.dot(high, matrix[1], preferred_element_type=jnp.float32)
    out += jnp.dot(low, matrix[0], preferred_element_type=jnp.float32)
    return out.reshape(rows.shape)


def times_conj(a, b):
    ar, ai, br, bi = a[..., :LANES], a[..., LANES:], b[..., :LANES], b[..., LANES:]
    return jnp.concatenate([ar * br + ai * bi, ar * bi - ai * br], axis=-1)


def times_plain(a, b):
    ar, ai, br, bi = a[..., :LANES], a[..., LANES:], b[..., :LANES], b[..., LANES:]
    return jnp.concatenate([ar * br - ai * bi, ar * bi + ai * br], axis=-1)


def mixing(
    peers,
    scale,
    query,
    key,
    value,
    grad,
    taps_in,
    forward_in,
    inverse_in,
    twist_in,
    diagonal_in,
    gate,
    mixed_out,
    query_grad,
    back,
    filter_out,
    conv,
    taps,
    forward,
    inverse,
    twist,
    diagonal,
    sent,
    got,
    replied,
    packed,
    wide,
    filter_spec,
    mixed_spec,
    grad_spec,
    term,
    term_got,
    half,
    half_got,
    load_sem,
    send_sem,
    recv_sem,
    term_sem,
    half_sem,
):
    me = lax.axis_index("ctx")
    dp = lax.axis_index("dp")
    line, side = dp // 2, dp % 2
    channels = taps.shape[0]

    barrier = pltpu.get_barrier_semaphore()

    loads = [
        pltpu.make_async_copy(source, target, load_sem.at[n])
        for n, (source, target) in enumerate(
            [
                (key, gate.at[0]),
                (value, gate.at[1]),
                (query, gate.at[2]),
                (grad, gate.at[3]),
                (taps_in, taps),
                (forward_in, forward),
                (inverse_in, inverse),
                (twist_in, twist),
                (diagonal_in, diagonal),
            ]
        )
    ]
    for load in loads[:2] + loads[8:]:
        load.start()

    for i in range(1, peers):
        pl.semaphore_signal(barrier, inc=1, device_id={"ctx": lax.rem(me + i, peers)}, device_id_type=MESH)
    for i in range(1, 4):
        pl.semaphore_signal(
            barrier, inc=1, device_id={"dp": lax.rem(line + i, 4) * 2 + side}, device_id_type=MESH
        )
    pl.semaphore_signal(barrier, inc=1, device_id={"dp": line * 2 + 1 - side}, device_id_type=MESH)

    def gated(first, second, slot):
        def body(t, carry):
            lanes = pl.ds(pl.multiple_of(t * LANES, LANES), LANES)
            product = gate[first, :, lanes].astype(jnp.float32) * gate[second, :, lanes].astype(jnp.float32)
            flipped = lax.dot_general(
                diagonal[...],
                product.astype(jnp.bfloat16),
                (((1,), (1,)), ((), ())),
                preferred_element_type=jnp.float32,
            ).astype(jnp.bfloat16)
            sent[slot, pl.ds(2 * t, 2)] = flipped.reshape(2, LANES // 2, LANES)
            return carry

        grouped(peers // 2, 4, body)
        got[slot, me] = sent[slot, me]

    def scatter(source, target, n):
        def body(i, carry):
            peer = lax.rem(me + i, peers)
            pltpu.make_async_remote_copy(
                src_ref=source.at[peer],
                dst_ref=target.at[me],
                send_sem=send_sem.at[n],
                recv_sem=recv_sem.at[n],
                device_id={"ctx": peer},
                device_id_type=MESH,
            ).start()
            return carry

        for i in range(1, peers):
            body(i, 0)

    def whole(source, target, n):
        part = pl.ds(0, peers - 1)
        return pltpu.make_async_remote_copy(
            src_ref=source.at[part],
            dst_ref=target.at[part],
            send_sem=send_sem.at[n],
            recv_sem=recv_sem.at[n],
            device_id={"ctx": lax.rem(me + 1, peers)},
            device_id_type=MESH,
        )

    loads[0].wait()
    loads[1].wait()
    loads[8].wait()
    for load in loads[2:8]:
        load.start()
    gated(0, 1, 0)
    pl.semaphore_wait(barrier, peers - 1 + 4)
    scatter(sent.at[0], got.at[0], 0)
    loads[2].wait()
    loads[3].wait()
    gated(2, 3, 1)
    scatter(sent.at[1], got.at[1], 1)
    for load in loads[4:8]:
        load.wait()

    analyse(lambda j, rows: taps[rows, j * LANES : (j + 1) * LANES], twist, packed, channels)

    def filter_step(k):
        filter_spec[k] = times(packed[k], forward)

    chunks(filter_step)

    def convolve(slot, spectrum, product, answer):
        whole(sent.at[slot], got.at[slot], slot).wait_recv()
        analyse(lambda j, rows: got[slot, j, rows, :].astype(jnp.float32), twist, packed, channels)

        def step(k):
            spec = times(packed[k], forward)
            spectrum[k] = spec
            wide[k] = times(product(filter_spec[k], spec), inverse)

        chunks(step)

        def write(j, rows, values):
            replied[slot, j, rows, :] = values.astype(jnp.bfloat16)

        synthesise(wide, twist, write, channels)
        answer[me] = replied[slot, me]
        scatter(replied.at[slot], answer, slot + 2)

    convolve(0, mixed_spec, times_plain, conv)
    convolve(1, grad_spec, times_conj, back)

    def term_step(k):
        wide[k] = times(times_conj(mixed_spec[k], grad_spec[k]), inverse)

    chunks(term_step)

    def write_term(j, rows, values):
        term[j, rows, :] = values.astype(jnp.bfloat16)

    synthesise(wide, twist, write_term, channels)

    hops = []
    for i in range(1, 4):
        other = lax.rem(line + i, 4)
        hops.append(
            pltpu.make_async_remote_copy(
                src_ref=term.at[pl.ds(other * 8, 8)],
                dst_ref=term_got.at[i - 1],
                send_sem=term_sem.at[i - 1],
                recv_sem=term_sem.at[i + 2],
                device_id={"dp": other * 2 + side},
                device_id_type=MESH,
            )
        )
    for hop in hops:
        hop.start()

    def total(which):
        mine = term[pl.ds(line * 8 + which * 4, 4)].astype(jnp.float32)
        for i in range(3):
            mine += term_got[i, pl.ds(which * 4, 4)].astype(jnp.float32)
        return mine

    for hop in hops:
        hop.wait_recv()
    half[...] = total(1 - side).astype(jnp.bfloat16)
    cross = pltpu.make_async_remote_copy(
        src_ref=half,
        dst_ref=half_got,
        send_sem=half_sem.at[0],
        recv_sem=half_sem.at[1],
        device_id={"dp": line * 2 + 1 - side},
        device_id_type=MESH,
    )
    cross.start()
    kept = total(side)
    for j in range(4):
        filter_out[:, j * LANES : (j + 1) * LANES] = kept[j]

    whole(replied.at[0], conv, 2).wait_recv()

    def conv_tile(t, carry):
        lanes = pl.ds(pl.multiple_of(t * LANES, LANES), LANES)
        columns = turned_over(diagonal[...], conv[pl.ds(2 * t, 2)].reshape(LANES, LANES))
        mixed_out[:, lanes] = (gate[2, :, lanes].astype(jnp.float32) * columns).astype(jnp.bfloat16)
        query_grad[:, lanes] = (gate[3, :, lanes].astype(jnp.float32) * columns).astype(jnp.bfloat16)
        return carry

    grouped(peers // 2, 4, conv_tile)
    cross.wait_recv()
    for j in range(4):
        lanes = slice(j * LANES, (j + 1) * LANES)
        filter_out[:, lanes] = (filter_out[:, lanes] + half_got[j].astype(jnp.float32)) * scale
    for slot in range(2):
        whole(sent.at[slot], got.at[slot], slot).wait_send()
    whole(replied.at[0], conv, 2).wait_send()
    for hop in hops:
        hop.wait_send()
    cross.wait_send()
    whole(replied.at[1], back, 3).wait()


def turned_over(identity, rows):
    return lax.dot_general(identity, rows, (((1,), (1,)), ((), ())), preferred_element_type=jnp.float32)


def finish(steps, gate, mixed, query, back, total, mixed_out, query_grad, key_grad, value_grad, filter_grad, made, sem):
    block, width = mixed.shape
    rows = block // PIECES
    copies = []

    def send(source, target):
        copies.append(pltpu.make_async_copy(source, target, sem.at[len(copies)]))
        copies[-1].start()

    for held, out in ((mixed, mixed_out), (query, query_grad)):
        for n in range(PIECES):
            part = pl.ds(n * rows, rows)
            send(held.at[part], out.at[0, part])
    send(total, filter_grad)
    identity = lax.broadcasted_iota(jnp.int32, (block, block), 0) == lax.broadcasted_iota(
        jnp.int32, (block, block), 1
    )
    identity = identity.astype(jnp.float32).astype(jnp.bfloat16)
    owners = back.shape[0] // steps
    for n in range(steps):
        lanes = pl.ds(n * (width // steps), width // steps)
        columns = turned_over(identity, back[n * owners : (n + 1) * owners].reshape(-1, block))
        for slot, factor, out in ((0, 1, key_grad), (1, 0, value_grad)):
            made[slot, :, lanes] = (columns * gate[factor, :, lanes].astype(jnp.float32)).astype(jnp.bfloat16)
            send(made.at[slot, :, lanes], out.at[0, :, lanes])
    for copy in copies:
        copy.wait()


def shards(query_gate, key_gate, value_in, out_grad, filter_taps):
    _, block, width = query_gate.shape
    channels, seq_len = filter_taps.shape
    peers = lax.axis_size("ctx")
    parts = lax.axis_size("dp")
    forward, inverse, twist, diagonal = tables()
    in_hbm = pl.BlockSpec(memory_space=pltpu.HBM)
    in_vmem = pl.BlockSpec(memory_space=pltpu.VMEM)
    planes = (peers, channels, LANES)
    spectrum = pltpu.VMEM((BINS, channels, 2 * LANES), jnp.float32)
    share = seq_len // parts
    tokens = jax.ShapeDtypeStruct(query_gate.shape, jnp.bfloat16)
    filter_share = jax.ShapeDtypeStruct((channels, share), jnp.float32)
    held = pl.pallas_call(
        functools.partial(mixing, peers, (seq_len * parts) ** (-0.5)),
        out_shape=(
            pltpu.VMEM((4, block, width), jnp.bfloat16),
            pltpu.VMEM((block, width), jnp.bfloat16),
            pltpu.VMEM((block, width), jnp.bfloat16),
            pltpu.VMEM(planes, jnp.bfloat16),
            pltpu.VMEM(filter_share.shape, filter_share.dtype),
        ),
        in_specs=[in_hbm] * 9,
        out_specs=(in_vmem,) * 5,
        scratch_shapes=[
            pltpu.VMEM(planes, jnp.bfloat16),
            pltpu.VMEM((channels, seq_len), jnp.float32),
            pltpu.VMEM((2, 2 * LANES, 2 * LANES), jnp.bfloat16),
            pltpu.VMEM((2, 2 * LANES, 2 * LANES), jnp.bfloat16),
            pltpu.VMEM((BINS, 2 * LANES), jnp.float32),
            pltpu.VMEM((LANES, LANES), jnp.bfloat16),
            pltpu.VMEM((2,) + planes, jnp.bfloat16),
            pltpu.VMEM((2,) + planes, jnp.bfloat16),
            pltpu.VMEM((2,) + planes, jnp.bfloat16),
            spectrum,
            spectrum,
            spectrum,
            spectrum,
            spectrum,
            pltpu.VMEM(planes, jnp.bfloat16),
            pltpu.VMEM((3, 8, channels, LANES), jnp.bfloat16),
            pltpu.VMEM((4, channels, LANES), jnp.bfloat16),
            pltpu.VMEM((4, channels, LANES), jnp.bfloat16),
            pltpu.SemaphoreType.DMA((9,)),
            pltpu.SemaphoreType.DMA((4,)),
            pltpu.SemaphoreType.DMA((4,)),
            pltpu.SemaphoreType.DMA((6,)),
            pltpu.SemaphoreType.DMA((2,)),
        ],
        compiler_params=pltpu.CompilerParams(
            collective_id=0, has_side_effects=True, vmem_limit_bytes=32 << 20
        ),
        name="mixing",
    )(
        *(
            pltpu.with_memory_space_constraint(a, pltpu.HBM)
            for a in (
                query_gate[0],
                key_gate[0],
                value_in[0],
                out_grad[0],
                filter_taps,
                forward,
                inverse,
                twist,
                diagonal,
            )
        )
    )

    steps = 2
    return pl.pallas_call(
        functools.partial(finish, steps),
        out_shape=tuple(pltpu.HBM(a.shape, a.dtype) for a in (tokens,) * 4 + (filter_share,)),
        in_specs=[in_vmem] * 5,
        out_specs=(in_hbm,) * 5,
        scratch_shapes=[
            pltpu.VMEM((2, block, width), jnp.bfloat16),
            pltpu.SemaphoreType.DMA((2 * PIECES + 1 + 2 * steps,)),
        ],
        compiler_params=pltpu.CompilerParams(vmem_limit_bytes=16 << 20),
        name="finish",
    )(*(pltpu.with_memory_space_constraint(a, pltpu.VMEM) for a in held))


def solution(mesh):
    placed = (
        P("dp", "ctx", None),
        P("dp", "ctx", None),
        P("dp", "ctx", None),
        P("dp", "ctx", None),
        P("ctx", None),
    )
    return jax.shard_map(
        shards,
        mesh=mesh,
        in_specs=placed,
        out_specs=(
            P("dp", "ctx", None),
            P("dp", "ctx", None),
            P("dp", "ctx", None),
            P("dp", "ctx", None),
            P("ctx", "dp"),
        ),
        check_vma=False,
    )
```
